128 devices in a mesh: ctx: 8 (over z, core), exp: 16 (over x, y).
Axes of the slice: x: 4, y: 4, z: 4, core: 2. Of those that a mesh axis runs over, the one named last changes fastest.
Arguments:
- queries: bfloat16 [16, 1024, 4096], P('exp', 'ctx'), may hold values from -100 to 100
- keys: bfloat16 [16, 1024, 256], P('exp', 'ctx'), may hold values from -12 to 12
- values: bfloat16 [16, 1024, 256], P('exp', 'ctx'), may hold values from -6 to 6
- residual: bfloat16 [16, 1024, 4096], P('exp', 'ctx'), may hold values from -6 to 6
- out_weight: bfloat16 [4096, 4096], P('ctx'), may hold values from -0.09375 to 0.09375
- norm_gain: float32 [4096], replicated, may hold values from 0.5 to 1.5
- expert_ids: int32 [16, 1024, 8], P('exp', 'ctx'), may hold values from 0 to 127, as said below
- gate_weights: float32 [16, 1024, 8], P('exp', 'ctx'), may hold values from 0.2 to 1
- slots: int32 [16, 1024, 8], P('exp', 'ctx'), may hold values from -1 to 3, as said below
- w_gate: bfloat16 [16, 4096, 1536], P('exp', None, 'ctx'), may hold values from -0.09375 to 0.09375
- w_up: bfloat16 [16, 4096, 1536], P('exp', None, 'ctx'), may hold values from -0.09375 to 0.09375
- w_down: bfloat16 [16, 1536, 4096], P('exp', 'ctx'), may hold values from -0.15625 to 0.15625
Outputs:
- attended: bfloat16 [16, 1024, 4096], P('exp', 'ctx')
- layer_out: bfloat16 [16, 1024, 4096], P('exp', 'ctx')
The draws below stay inside these ranges and needn't reach their ends.
Inputs may be any that keep to these rules, and one draw needn't show every extreme that they name: `expert_ids`: each token names 8 different experts. Within one block of 128 positions, the choices of each expert below 16, taken in order of position and then of k, get slots 0, 1, 2 and so on; choices past 4 - 1 and choices of experts 16 or above get -1. Some expert fills all 4 slots in every block.
All inputs are finite; a program needn't handle non-finite values.
Results may differ from the reference program's by a relative error of at most 0.015.
Values may be sent and summed in bfloat16 or wider, within the bound.
A program may use at most 64 MiB of HBM per device.

```python
import jax
import jax.numpy as jnp
from jax import lax

D = 4096
HD = 128
QH = 32
KVH = 2
FF = 1536
ROUTED = 128
EXPERTS_PER_TOKEN = 8
TOK_DEV = 128
LEN = 1024
SEQS = 16
EXPERTS = 16
CAP = 4
GROUP = 16
N_CTX = 8


def shared_keys(key):
    first = jax.random.fold_in(key, 0)
    base = 1.3 * jax.random.normal(first, (SEQS, LEN, KVH, HD), jnp.float32)
    return base


def draw_queries(key, part):
    key = jax.random.fold_in(key, 5)
    noise = 1.3 * jax.random.normal(key, (SEQS, LEN, QH, HD), jnp.float32)
    return noise.reshape(SEQS, LEN, QH * HD).astype(jnp.bfloat16)


def draw_keys(key, part):
    base = shared_keys(key)
    return base.reshape(SEQS, LEN, KVH * HD).astype(jnp.bfloat16)


def routing(key):
    rows = SEQS * LEN
    blocks = rows // TOK_DEV
    first, second, third, fourth = jax.random.split(key, 4)
    router_logits = jax.random.randint(first, (rows, ROUTED), 0, 1 << 20) * ROUTED + jnp.arange(ROUTED, dtype=jnp.int32)[None, :]
    block_hot = jax.random.randint(second, (blocks,), 0, EXPERTS)
    shared_hot_mask = jax.random.randint(fourth, (), 0, EXPERTS)
    order = jax.random.randint(third, (blocks, TOK_DEV), 0, 1 << 20) * TOK_DEV + jnp.arange(TOK_DEV, dtype=jnp.int32)[None, :]
    ranks = jnp.argsort(jnp.argsort(order, axis=1), axis=1)
    first_selection = (ranks < TOK_DEV // 2).reshape(rows)
    second_selection = (ranks >= TOK_DEV - TOK_DEV // 4).reshape(rows)
    favored_row = jnp.repeat(block_hot, TOK_DEV)
    column_indices = jnp.arange(ROUTED, dtype=jnp.int32)[None, :]
    extra_logit = jnp.where(first_selection[:, None] & (column_indices == favored_row[:, None]), 1 << 28, 0)
    extra_logit = extra_logit + jnp.where(second_selection[:, None] & (column_indices == shared_hot_mask), 1 << 28, 0)
    identifiers = lax.top_k(router_logits + extra_logit, EXPERTS_PER_TOKEN)[1].astype(jnp.int32)
    flat = identifiers.reshape(blocks, TOK_DEV * EXPERTS_PER_TOKEN)
    match = (flat[..., None] == jnp.arange(EXPERTS, dtype=jnp.int32)).astype(jnp.int32)
    seen = jnp.cumsum(match, axis=1) - 1
    rank = jnp.sum(match * seen, axis=-1)
    inside = flat < EXPERTS
    slot = jnp.where(inside & (rank < CAP), rank, -1)
    return (identifiers.reshape(SEQS, LEN, EXPERTS_PER_TOKEN), slot.reshape(SEQS, LEN, EXPERTS_PER_TOKEN).astype(jnp.int32))


def draw_expert_ids(key, part):
    identifiers, slot = routing(key)
    return identifiers


def draw_slots(key, part):
    identifiers, slot = routing(key)
    return slot


def steps_of(key, dims, pieces, smallest, top_value):
    def one(axis_at, shards_of):
        draws = jax.random.uniform(jax.random.fold_in(jax.random.fold_in(key, 6), axis_at), (shards_of,), jnp.float32, smallest / len(pieces), top_value / len(pieces))
        return jnp.repeat(jnp.exp(draws), dims[axis_at] // shards_of).reshape((-1,) + (1,) * (len(dims) - axis_at - 1))

    factor_of = one(*pieces[0])
    for cut in pieces[1:]:
        factor_of = factor_of * one(*cut)
    return factor_of


def gaussian(stream_key, dims, spread, most, shards=(), kind=jnp.bfloat16):
    array = jax.random.normal(stream_key, dims, jnp.float32) * spread
    if len(shards) > 0:
        array = steps_of(stream_key, dims, shards, -0.22, 0.18) * array
    return jnp.clip(array, min=-most, max=most).astype(kind)


def setup_inputs(seed: int = 0) -> dict:
    key_list = jax.random.split(jax.random.key(seed), 13)
    return {
        "queries": draw_queries(jax.random.fold_in(key_list[12], 71), 0),
        "keys": draw_keys(jax.random.fold_in(key_list[12], 71), 0),
        "values": gaussian(key_list[2], (SEQS, LEN, KVH * HD), 1.0, 6.0, ((0, 16), (1, 8))),
        "residual": gaussian(key_list[3], (SEQS, LEN, D), 1.0, 6.0, ((0, 16), (1, 8))),
        "out_weight": gaussian(key_list[4], (QH * HD, D), (QH * HD) ** -0.5, 0.09375, ((0, 8),)),
        "norm_gain": jnp.clip(1.0 + 0.1 * jax.random.normal(key_list[5], (D,), jnp.float32), 0.5, 1.5),
        "expert_ids": draw_expert_ids(jax.random.fold_in(key_list[12], 71), 0),
        "gate_weights": jnp.clip(0.2 + 0.8 * jax.random.uniform(key_list[7], (SEQS, LEN, EXPERTS_PER_TOKEN), jnp.float32) ** steps_of(key_list[7], (SEQS, LEN, EXPERTS_PER_TOKEN), ((0, 16), (1, 8)), -0.2, 0.2), 0.2, 1.0),
        "slots": draw_slots(jax.random.fold_in(key_list[12], 71), 0),
        "w_gate": gaussian(key_list[9], (EXPERTS, D, FF), D ** -0.5, 0.09375, ((0, 16), (2, 8))),
        "w_up": gaussian(key_list[10], (EXPERTS, D, FF), D ** -0.5, 0.09375, ((0, 16), (2, 8))),
        "w_down": gaussian(key_list[11], (EXPERTS, FF, D), FF ** -0.5, 0.15625, ((0, 16), (1, 8))),
    }


def attend_one(args):
    q_seq, k_seq, v_seq = args
    qh = q_seq.reshape(LEN, KVH, GROUP, HD).astype(jnp.float32)
    kh = k_seq.reshape(LEN, KVH, HD).astype(jnp.float32)
    vh = v_seq.reshape(LEN, KVH, HD).astype(jnp.float32)
    router_logits = jnp.einsum('qhgd,khd->hgqk', qh, kh) * HD ** (-0.5)
    where_q = jnp.arange(LEN)[:, None]
    where_k = jnp.arange(LEN)[None, :]
    router_logits = jnp.where(where_q >= where_k, router_logits, -jnp.inf)
    top = lax.optimization_barrier(jnp.max(router_logits, axis=-1, keepdims=True))
    weights = jnp.exp(router_logits - top)
    probs = (weights / lax.optimization_barrier(jnp.sum(weights, axis=-1, keepdims=True))).astype(jnp.bfloat16)
    mixed = jnp.einsum('hgqk,khd->qhgd', probs.astype(jnp.float32), vh)
    return mixed.astype(jnp.bfloat16).reshape(LEN, QH * HD)

def rounded(part):
    return lax.optimization_barrier(part.astype(jnp.bfloat16)).astype(jnp.float32)

def expert_one(args):
    rows, gate_w, up_w, down_w = args
    share = FF // N_CTX
    total = jnp.zeros((rows.shape[0], D), jnp.float32)
    for group in range(N_CTX):
        low = group * share
        gate = jnp.dot(rows, gate_w[:, low:low + share], preferred_element_type=jnp.float32)
        upper = jnp.dot(rows, up_w[:, low:low + share], preferred_element_type=jnp.float32)
        hidden = (jax.nn.silu(gate) * upper).astype(jnp.bfloat16)
        part = jnp.dot(hidden, down_w[low:low + share], preferred_element_type=jnp.float32)
        total = total + rounded(part)
    return total.astype(jnp.bfloat16)

def reference(queries, keys, values, residual, out_weight, norm_gain, expert_ids, gate_weights, slots, w_gate, w_up, w_down):
    heads_out = lax.map(attend_one, (queries, keys, values)).reshape(SEQS * LEN, QH * HD)
    share = QH * HD // N_CTX
    proj = jnp.zeros((SEQS * LEN, D), jnp.float32)
    for group in range(N_CTX):
        low = group * share
        part = jnp.dot(heads_out[:, low:low + share], out_weight[low:low + share], preferred_element_type=jnp.float32)
        proj = proj + rounded(part)
    attended = (residual.reshape(SEQS * LEN, D).astype(jnp.float32) + proj).astype(jnp.bfloat16)
    stream = attended.astype(jnp.float32)
    scale = lax.rsqrt(lax.optimization_barrier(jnp.mean(stream * stream, axis=-1, keepdims=True)) + 1e-06)
    normed = (stream * scale * norm_gain).astype(jnp.bfloat16)
    blocks = SEQS * N_CTX
    width = EXPERTS * CAP
    identifiers = expert_ids.reshape(blocks, TOK_DEV, EXPERTS_PER_TOKEN)
    slot = slots.reshape(blocks, TOK_DEV, EXPERTS_PER_TOKEN)
    dest = identifiers * CAP + slot
    valid = slot >= 0
    route = ((dest[..., None] == jnp.arange(width, dtype=jnp.int32)) & valid[..., None]).astype(jnp.float32)
    placing = lax.optimization_barrier(jnp.sum(route, axis=2))
    rows = normed.reshape(blocks, TOK_DEV, D).astype(jnp.float32)
    dispatched = jnp.einsum('bte,btd->bed', placing, rows).astype(jnp.bfloat16)
    per_expert = dispatched.reshape(blocks, EXPERTS, CAP, D).transpose(1, 0, 2, 3).reshape(EXPERTS, blocks * CAP, D)
    expert_out = lax.map(expert_one, (per_expert, w_gate, w_up, w_down))
    back = expert_out.reshape(EXPERTS, blocks, CAP, D).transpose(1, 0, 2, 3).reshape(blocks, width, D)
    combine = jnp.einsum('btke,btk->bte', route, gate_weights.reshape(blocks, TOK_DEV, EXPERTS_PER_TOKEN))
    moe = jnp.einsum('bte,bed->btd', combine, back.astype(jnp.float32), precision=lax.Precision.HIGHEST)
    layer_out = (stream + moe.reshape(SEQS * LEN, D)).astype(jnp.bfloat16)
    return (attended.reshape(SEQS, LEN, D), layer_out.reshape(SEQS, LEN, D))
```

```python
import functools

import jax
import jax.numpy as jnp
from jax import lax
from jax.experimental import pallas as pl
from jax.experimental.pallas import tpu as pltpu
from jax.sharding import PartitionSpec as P

D = 4096
HD = 128
QH = 32
TOK = 128
NZ = 4
HEADS = QH // NZ
HW = HEADS * HD
SEQ = 1024
FF_DEV = 192
FF_CHIP = 2 * FF_DEV
K_DEV = 512
CAP = 4
ROWS = 64
SCALE_COLS = 128
NCH = 4
CW = D // NCH
DX = D + SCALE_COLS
F32 = jnp.float32
BF16 = jnp.bfloat16
MESH = pl.DeviceIdType.MESH

NT = (((1,), (1,)), ((), ()))
TN = (((0,), (0,)), ((), ()))


def cols(j):
    return pl.ds(j * CW, CW)


def xcols(j):
    return pl.ds(j * CW, CW + (SCALE_COLS if j == NCH - 1 else 0))


_count = 0


def _take(n):
    global _count
    first = _count
    _count += n
    return first


S_Q = _take(4)
S_KV = _take(8)
S_FWD = _take(4)
S_W = _take(1)
S_EW = _take(3)
S_RELAY1 = _take(NCH)
S_PLUS1 = _take(NCH)
S_MINUS1 = _take(NCH)
S_X1 = _take(4 * NCH)
S_Y1 = _take(4 * NCH)
S_G1 = _take(NCH)
S_G2 = _take(NCH)
S_G3 = _take(NCH)
S_RELAY2 = _take(NCH)
S_PLUS2 = _take(NCH)
S_MINUS2 = _take(NCH)
S_Y2 = _take(4 * NCH)
S_X2 = _take(4 * NCH)
N_SEM = _count

L_Q = 0
L_K = 1
L_V = 2
L_W = 3
L_G = 4
L_U = 5
L_D = 6
L_RES = 7
L_ATT = 8
L_OUT = L_ATT + NCH
N_LOC = L_OUT + NCH


def layer(
    q_in, k_in, v_in, res_in, w_in, g_in, u_in, d_in, gain_ref, ids_ref, gates_ref, slots_ref,
    att_out, lay_out,
    qb, kv, wb, gub, db, res, heads, part, relay, plus, minus, att, place, comb_hi, comb_lo, gain_b,
    disp, xr, yb, xall, acc, hid, ypart, relay2, plus2, minus2, yfin, yr, xb, eb,
    ssem, rsem, lsem,
):
    ctx = lax.axis_index("ctx")
    ex = lax.axis_index("exp")
    z, c = ctx // 2, ctx % 2
    x, y = ex // 4, ex % 4

    def at_z(d):
        return (lax.rem(z + d + NZ, NZ) * 2 + c, ex)

    def at_x(d):
        return (ctx, lax.rem(x + d + 4, 4) * 4 + y)

    def at_y(d):
        return (ctx, x * 4 + lax.rem(y + d + 4, 4))

    other = (z * 2 + 1 - c, ex)

    barrier = pltpu.get_barrier_semaphore()
    peers = [other] + [at(d) for at in (at_z, at_x, at_y) for d in (1, 2, 3)]
    for peer in peers:
        pl.semaphore_signal(barrier, inc=1, device_id=peer, device_id_type=MESH)

    def local(src, dst, n):
        return pltpu.make_async_copy(src, dst, lsem.at[n])

    sent = []

    def remote(src, dst, n, dev):
        return pltpu.make_async_remote_copy(
            src_ref=src, dst_ref=dst, send_sem=ssem.at[n], recv_sem=rsem.at[n],
            device_id=dev, device_id_type=MESH,
        )

    def send(src, dst, n, dev):
        copy = remote(src, dst, n, dev)
        copy.start()
        sent.append(copy)
        return copy

    my_head = (z // 2) * HD
    mine = (2 * z + c) * TOK
    my_rows = pl.ds(pl.multiple_of(mine, TOK), TOK)
    own_k = local(k_in.at[:, pl.ds(pl.multiple_of(my_head, HD), HD)], kv.at[my_rows, pl.ds(0, HD)], L_K)
    own_v = local(v_in.at[:, pl.ds(pl.multiple_of(my_head, HD), HD)], kv.at[my_rows, pl.ds(HD, HD)], L_V)
    own_q = local(q_in.at[:, pl.ds(pl.multiple_of(z * HW, HW), HW)], qb.at[0], L_Q)
    w_rows = pl.ds(pl.multiple_of(c * K_DEV, K_DEV), K_DEV)
    own_w = local(w_in, wb.at[w_rows], L_W)
    g_rows = pl.ds(pl.multiple_of(c * FF_DEV, FF_DEV), FF_DEV)
    u_rows = pl.ds(pl.multiple_of(FF_CHIP + c * FF_DEV, FF_DEV), FF_DEV)
    own_g = local(g_in, gub.at[g_rows], L_G)
    own_u = local(u_in, gub.at[u_rows], L_U)
    own_d = local(d_in, db.at[g_rows], L_D)
    own_res = local(res_in, res, L_RES)
    for copy in (own_k, own_v, own_q, own_w, own_res, own_g, own_u, own_d):
        copy.start()

    pl.semaphore_wait(barrier, len(peers))

    kv_copies = {}
    for d in (2, 1, 3):
        head = (lax.rem(z + d, NZ) // 2) * HD
        lanes = pl.ds(pl.multiple_of(head, HD), HD)
        kv_copies[d] = (
            send(k_in.at[:, lanes], kv.at[my_rows, pl.ds(0, HD)], S_KV + 2 * d, at_z(d)),
            send(v_in.at[:, lanes], kv.at[my_rows, pl.ds(HD, HD)], S_KV + 2 * d + 1, at_z(d)),
        )
    for d in (2, 1, 3):
        lanes = pl.ds(pl.multiple_of(lax.rem(z + d, NZ) * HW, HW), HW)
        send(q_in.at[:, lanes], qb.at[d], S_Q + d, at_z(d))
    w_copy = send(w_in, wb.at[w_rows], S_W, other)

    kv[:, pl.ds(2 * HD, HD)] = jnp.ones((SEQ, HD), BF16)
    ids = ids_ref[...]
    slots = slots_ref[...]
    gates = gates_ref[...]
    dest = ((ids // 4 - x) & 3) * 16 + ((ids & 3) - y & 3) * 4 + slots
    dest = jnp.where(slots >= 0, dest, -1)
    row = lax.broadcasted_iota(jnp.int32, (ROWS, TOK), 0)
    placing = jnp.zeros((ROWS, TOK), F32)
    combine = jnp.zeros((ROWS, TOK), F32)
    for k in range(8):
        hit = row == dest[k : k + 1]
        placing += jnp.where(hit, 1.0, 0.0)
        combine += jnp.where(hit, gates[k : k + 1], 0.0)
    place[...] = placing.astype(BF16)
    high = combine.astype(BF16)
    comb_hi[...] = high
    comb_lo[...] = (combine - high.astype(F32)).astype(BF16)
    gain_b[...] = jnp.broadcast_to(gain_ref[...], (8, D))

    own_k.wait()
    own_v.wait()
    kv_lanes = pl.ds(0, 2 * HD)
    fwd = [send(kv.at[my_rows, kv_lanes], kv.at[my_rows, kv_lanes], S_FWD, other)]
    for d in (1, 3, 2):
        kv_copies[d][0].wait_recv()
        kv_copies[d][1].wait_recv()
        rows = pl.ds(pl.multiple_of((lax.rem(z - d + NZ, NZ) * 2 + c) * TOK, TOK), TOK)
        fwd.append(send(kv.at[rows, kv_lanes], kv.at[rows, kv_lanes], S_FWD + d, other))
    ew_copies = (
        send(g_in, gub.at[g_rows], S_EW, other),
        send(u_in, gub.at[u_rows], S_EW + 1, other),
        send(d_in, db.at[g_rows], S_EW + 2, other),
    )
    for copy in fwd:
        copy.wait_recv()

    scale = HD**-0.5

    def attend(d, owner):
        limit = c * TOK + lax.broadcasted_iota(jnp.int32, (TOK, 2 * TOK), 0)
        seen = lax.broadcasted_iota(jnp.int32, (TOK, 2 * TOK), 1) <= limit
        for v in range(NZ):

            @pl.when(owner == v)
            def _():
                keys = kv[pl.ds(0, 2 * TOK * (v + 1)), pl.ds(0, HD)]
                vals = kv[pl.ds(0, 2 * TOK * (v + 1)), pl.ds(HD, 2 * HD)]
                for h in range(HEADS):
                    lanes = pl.ds(h * HD, HD)
                    s = lax.dot_general(qb[d, :, lanes], keys, NT, preferred_element_type=F32)
                    tail = jnp.where(seen, s[:, 2 * TOK * v :], -jnp.inf)
                    s = tail if v == 0 else jnp.concatenate([s[:, : 2 * TOK * v], tail], axis=1)
                    top = jnp.max(s, axis=1, keepdims=True)
                    p = jnp.exp((s - top) * scale).astype(BF16)
                    o = jnp.dot(p, vals, preferred_element_type=F32)
                    heads[:, lanes] = (o[:, :HD] / o[:, HD:]).astype(BF16)

    def relay_copy(src, dst, base, j):
        return remote(src, dst, base + j, at_z(1 if j % 2 == 0 else -1))

    def p_relay1(j):
        return relay_copy(part.at[2, :, cols(j)], relay.at[:, cols(j)], S_RELAY1, j)

    def p_plus1(j):
        return remote(part.at[1, :, cols(j)], plus.at[:, cols(j)], S_PLUS1 + j, at_z(-1))

    def p_minus1(j):
        return remote(part.at[3, :, cols(j)], minus.at[:, cols(j)], S_MINUS1 + j, at_z(1))

    def step_body(step, _):
        d = jnp.where(step == 0, 2, jnp.where(step == 1, 1, jnp.where(step == 2, 3, 0)))
        owner = lax.rem(z - d + NZ, NZ)

        @pl.when(step < 3)
        def _():
            pltpu.make_async_copy(qb.at[0], qb.at[d], rsem.at[S_Q + d]).wait()

        @pl.when(step == 3)
        def _():
            own_q.wait()

        attend(d, owner)

        @pl.when(step == 0)
        def _():
            own_w.wait()
            w_copy.wait_recv()

        for j in range(NCH):
            part[d, :, cols(j)] = jnp.dot(heads[...], wb[:, cols(j)], preferred_element_type=F32).astype(BF16)

            @pl.when(step == 0)
            def _():
                p_relay1(j).start()

            if j == 0:

                @pl.when(step == 1)
                def _():
                    p_plus1(j).start()

            if j == 1:

                @pl.when(step == 2)
                def _():
                    p_minus1(j).start()

        return 0

    lax.fori_loop(0, 4, step_body, 0)

    for j in range(NCH):
        joined, copy, direct = (3, p_minus1, p_plus1) if j % 2 == 0 else (1, p_plus1, p_minus1)
        p_relay1(j).wait_recv()
        part[joined, :, cols(j)] = (
            part[joined, :, cols(j)].astype(F32) + relay[:, cols(j)].astype(F32)
        ).astype(BF16)
        copy(j).start()
        if j >= 2:
            direct(j).start()
        sent.extend([p_relay1(j), p_plus1(j), p_minus1(j)])

    r = lax.broadcasted_iota(jnp.int32, (ROWS, ROWS), 0)
    s = lax.broadcasted_iota(jnp.int32, (ROWS, ROWS), 1)
    swap = jnp.where(((r // 16 == (s // 4) % 4) & ((r // 4) % 4 == s // 16)) & (r % 4 == s % 4), 1.0, 0.0).astype(BF16)

    own_res.wait()
    square = jnp.zeros((TOK, 1), F32)
    own_copies = []

    def x_send(j):
        return [
            remote(disp.at[pl.ds(16 * d, 16), xcols(j)], xr.at[pl.ds(16 * d, 16), xcols(j)], S_X1 + 4 * j + d, at_x(d))
            for d in (2, 1, 3)
        ]

    def y_send(j):
        return [
            remote(yb.at[pl.ds(16 * f, 16), xcols(j)], xall.at[pl.ds(16 * f, 16), xcols(j)], S_Y1 + 4 * j + f, at_y(f))
            for f in (2, 1, 3)
        ]

    def g1(j):
        return remote(xall.at[pl.ds(0, ROWS), xcols(j)], xall.at[pl.ds(ROWS, ROWS), xcols(j)], S_G1 + j, at_z(1))

    def g3(j):
        return remote(xall.at[pl.ds(0, ROWS), xcols(j)], xall.at[pl.ds(3 * ROWS, ROWS), xcols(j)], S_G3 + j, at_z(-1))

    def g2(j):
        slot, way = (1, 1) if j % 2 == 0 else (3, -1)
        return remote(
            xall.at[pl.ds(slot * ROWS, ROWS), xcols(j)], xall.at[pl.ds(2 * ROWS, ROWS), xcols(j)], S_G2 + j, at_z(way)
        )

    def start(copies):
        for copy in copies:
            copy.start()
            sent.append(copy)

    def attended_chunk(j, square):
        p_plus1(j).wait_recv()
        p_minus1(j).wait_recv()
        total = (
            part[0, :, cols(j)].astype(F32) + plus[:, cols(j)].astype(F32) + minus[:, cols(j)].astype(F32)
        )
        a = (res[:, cols(j)].astype(F32) + total).astype(BF16)
        att[:, cols(j)] = a
        copy = local(att.at[:, cols(j)], att_out.at[:, cols(j)], L_ATT + j)
        copy.start()
        own_copies.append(copy)
        a = a.astype(F32)
        square += jnp.sum(a * a, axis=1, keepdims=True)
        scaled = (a * gain_b[pl.ds(0, 1), cols(j)]).astype(BF16)
        rows = jnp.dot(place[...], scaled, preferred_element_type=F32).astype(BF16)
        disp[:, cols(j)] = rows
        xr[pl.ds(0, 16), cols(j)] = rows[:16]
        if j == NCH - 1:
            norm = lax.rsqrt(square * (1.0 / D) + 1e-06)
            norm = jnp.broadcast_to(norm, (TOK, SCALE_COLS))
            norm_hi = norm.astype(BF16).astype(F32)
            lane = lax.broadcasted_iota(jnp.int32, (TOK, SCALE_COLS), 1)
            both = jnp.where(lane < SCALE_COLS // 2, norm_hi, norm - norm_hi).astype(BF16)
            rows = jnp.dot(place[...], both, preferred_element_type=F32).astype(BF16)
            disp[:, pl.ds(D, SCALE_COLS)] = rows
            xr[pl.ds(0, 16), pl.ds(D, SCALE_COLS)] = rows[:16]
        start(x_send(j))
        return square

    def turn_chunk(j):
        for copy in x_send(j):
            copy.wait_recv()
        rows = jnp.dot(swap, xr[:, xcols(j)], preferred_element_type=F32).astype(BF16)
        yb[:, xcols(j)] = rows
        xall[pl.ds(0, 16), xcols(j)] = rows[:16]
        start(y_send(j))

    def gather_chunk(j):
        for copy in y_send(j):
            copy.wait_recv()
        start([g1(j), g3(j)])

    def pass_chunk(j):
        (g1(j) if j % 2 == 0 else g3(j)).wait_recv()
        start([g2(j)])

    def gate_up_chunk(j):
        (g3(j) if j % 2 == 0 else g1(j)).wait_recv()
        g2(j).wait_recv()
        prod = lax.dot_general(xall[:, cols(j)], gub[:, cols(j)], NT, preferred_element_type=F32)
        acc[...] = prod if j == 0 else acc[...] + prod

    for pair in range(NCH // 2):
        js = (2 * pair, 2 * pair + 1)
        for j in js:
            square = attended_chunk(j, square)
        for j in js:
            turn_chunk(j)
        for j in js:
            gather_chunk(j)

    own_g.wait()
    own_u.wait()
    own_d.wait()
    for copy in ew_copies:
        copy.wait_recv()
    for pair in range(NCH // 2):
        js = (2 * pair, 2 * pair + 1)
        for j in js:
            pass_chunk(j)
        for j in js:
            gate_up_chunk(j)

    sc = xall[:, pl.ds(D, SCALE_COLS)].astype(F32)
    sc = sc[:, 0:1] + sc[:, SCALE_COLS // 2 : SCALE_COLS // 2 + 1]
    gate = acc[:, pl.ds(0, FF_CHIP)] * sc
    upper = acc[:, pl.ds(FF_CHIP, FF_CHIP)] * sc
    hid[...] = (gate * jax.nn.sigmoid(gate) * upper).astype(BF16)

    def q_relay2(j):
        return relay_copy(ypart.at[pl.ds(2 * ROWS, ROWS), cols(j)], relay2.at[:, cols(j)], S_RELAY2, j)

    def q_plus2(j):
        return remote(ypart.at[pl.ds(ROWS, ROWS), cols(j)], plus2.at[:, cols(j)], S_PLUS2 + j, at_z(-1))

    def q_minus2(j):
        return remote(ypart.at[pl.ds(3 * ROWS, ROWS), cols(j)], minus2.at[:, cols(j)], S_MINUS2 + j, at_z(1))

    for j in range(NCH):
        ypart[:, cols(j)] = jnp.dot(hid[...], db[:, cols(j)], preferred_element_type=F32).astype(BF16)
        start([q_relay2(j)])
    start([q_plus2(0), q_minus2(1)])
    for j in range(NCH):
        joined, copy, direct = (3, q_minus2, q_plus2) if j % 2 == 0 else (1, q_plus2, q_minus2)
        q_relay2(j).wait_recv()
        rows = pl.ds(joined * ROWS, ROWS)
        ypart[rows, cols(j)] = (ypart[rows, cols(j)].astype(F32) + relay2[:, cols(j)].astype(F32)).astype(BF16)
        start([copy(j)])
        if j >= 2:
            start([direct(j)])

    def y_back(j):
        return [
            remote(yfin.at[pl.ds(16 * f, 16), cols(j)], yr.at[pl.ds(16 * f, 16), cols(j)], S_Y2 + 4 * j + f, at_y(-f))
            for f in (2, 1, 3)
        ]

    def x_back(j):
        return [
            remote(xb.at[pl.ds(16 * d, 16), cols(j)], eb.at[pl.ds(16 * d, 16), cols(j)], S_X2 + 4 * j + d, at_x(-d))
            for d in (2, 1, 3)
        ]

    def sum_chunk(j):
        q_plus2(j).wait_recv()
        q_minus2(j).wait_recv()
        rows = (
            ypart[pl.ds(0, ROWS), cols(j)].astype(F32) + plus2[:, cols(j)].astype(F32) + minus2[:, cols(j)].astype(F32)
        ).astype(BF16)
        yfin[:, cols(j)] = rows
        yr[pl.ds(0, 16), cols(j)] = rows[:16]
        start(y_back(j))

    def turn_back(j):
        for copy in y_back(j):
            copy.wait_recv()
        rows = jnp.dot(swap, yr[:, cols(j)], preferred_element_type=F32).astype(BF16)
        xb[:, cols(j)] = rows
        eb[pl.ds(0, 16), cols(j)] = rows[:16]
        start(x_back(j))

    def combine_chunk(j):
        for copy in x_back(j):
            copy.wait_recv()
        e = eb[:, cols(j)]
        moe = lax.dot_general(comb_hi[...], e, TN, preferred_element_type=F32)
        moe += lax.dot_general(comb_lo[...], e, TN, preferred_element_type=F32)
        plus[:, cols(j)] = (att[:, cols(j)].astype(F32) + moe).astype(BF16)
        copy = local(plus.at[:, cols(j)], lay_out.at[:, cols(j)], L_OUT + j)
        copy.start()
        own_copies.append(copy)

    for pair in range(NCH // 2):
        js = (2 * pair, 2 * pair + 1)
        for j in js:
            sum_chunk(j)
        for j in js:
            turn_back(j)
        for j in js:
            combine_chunk(j)

    for copy in own_copies:
        copy.wait()
    for copy in sent:
        copy.wait_send()


def shards(
    queries, keys, values, residual, out_weight, norm_gain, expert_ids, gate_weights, slots, w_gate, w_up, w_down
):
    out = jax.ShapeDtypeStruct((TOK, D), BF16)
    hbm = pl.BlockSpec(memory_space=pl.ANY)
    vmem = pl.BlockSpec(memory_space=pltpu.VMEM)

    def buf(*shape, dtype=BF16):
        return pltpu.VMEM(shape, dtype)

    attended, layer_out = pl.pallas_call(
        layer,
        out_shape=(out, out),
        in_specs=[hbm] * 8 + [vmem] * 4,
        out_specs=(hbm, hbm),
        scratch_shapes=[
            buf(NZ, TOK, HW),
            buf(SEQ, 3 * HD),
            buf(2 * K_DEV, D),
            buf(2 * FF_CHIP, D),
            buf(FF_CHIP, D),
            buf(TOK, D),
            buf(TOK, HW),
            buf(NZ, TOK, D),
            buf(TOK, D),
            buf(TOK, D),
            buf(TOK, D),
            buf(TOK, D),
            buf(ROWS, TOK),
            buf(ROWS, TOK),
            buf(ROWS, TOK),
            buf(8, D, dtype=F32),
            buf(ROWS, DX),
            buf(ROWS, DX),
            buf(ROWS, DX),
            buf(NZ * ROWS, DX),
            buf(NZ * ROWS, 2 * FF_CHIP, dtype=F32),
            buf(NZ * ROWS, FF_CHIP),
            buf(NZ * ROWS, D),
            buf(ROWS, D),
            buf(ROWS, D),
            buf(ROWS, D),
            buf(ROWS, D),
            buf(ROWS, D),
            buf(ROWS, D),
            buf(ROWS, D),
            pltpu.SemaphoreType.DMA((N_SEM,)),
            pltpu.SemaphoreType.DMA((N_SEM,)),
            pltpu.SemaphoreType.DMA((N_LOC,)),
        ],
        compiler_params=pltpu.CompilerParams(collective_id=0, has_side_effects=True, vmem_limit_bytes=56 << 20),
        name="decoder_layer",
    )(
        queries[0], keys[0], values[0], residual[0], out_weight,
        w_gate[0].T, w_up[0].T, w_down[0], norm_gain[None],
        expert_ids[0].T, gate_weights[0].T, slots[0].T,
    )
    return attended[None], layer_out[None]


def solution(mesh):
    rows = P("exp", "ctx", None)
    placed = (rows, rows, rows, rows, P("ctx", None), P(), rows, rows, rows,
              P("exp", None, "ctx"), P("exp", None, "ctx"), rows)
    return jax.shard_map(shards, mesh=mesh, in_specs=placed, out_specs=(rows, rows), check_vma=False)
```

```python
import functools

import jax
import jax.numpy as jnp
from jax import lax
from jax.experimental import pallas as pl
from jax.experimental.pallas import tpu as pltpu
from jax.sharding import PartitionSpec as P

D = 4096
HD = 128
QH = 32
TOK = 128
NZ = 4
HEADS = QH // NZ
HW = HEADS * HD
SEQ = 1024
FF_DEV = 192
FF_CHIP = 2 * FF_DEV
K_DEV = 512
CAP = 4
ROWS = 64
SCALE_COLS = 128
NCH = 4
CW = D // NCH
DX = D + SCALE_COLS
HALF = D // 2
QW = HALF // 4
BLOCKS = 16
STACK = 4 * ROWS
F32 = jnp.float32
BF16 = jnp.bfloat16
MESH = pl.DeviceIdType.MESH

NT = (((1,), (1,)), ((), ()))


def cols(j):
    return pl.ds(j * CW, CW)


def xcols(j):
    return pl.ds(j * CW, CW + (SCALE_COLS if j == NCH - 1 else 0))


def qcols(p):
    return pl.ds(p * QW, QW + (SCALE_COLS if p == 1 else 0))


_count = 0


def _take(n):
    global _count
    first = _count
    _count += n
    return first


S_Q = _take(4)
S_KV = _take(8)
S_FWD = _take(4)
S_W = _take(1)
S_EW = _take(3)
S_RELAY1 = _take(NCH)
S_PLUS1 = _take(NCH)
S_MINUS1 = _take(NCH)
S_OUT = _take(2 * BLOCKS)
S_G1 = _take(NCH)
S_G2 = _take(NCH)
S_G3 = _take(NCH)
S_RELAY2 = _take(NCH)
S_PLUS2 = _take(NCH)
S_MINUS2 = _take(NCH)
S_BACK = _take(2 * BLOCKS)
N_SEM = _count

L_Q = 0
L_K = 1
L_V = 2
L_W = 3
L_G = 4
L_U = 5
L_D = 6
L_RES = 7
L_ATT = 8
L_OUT = L_ATT + NCH
N_LOC = L_OUT + NCH


def layer(
    q_in, k_in, v_in, res_in, w_in, g_in, u_in, d_in, gain_ref, ids_ref, gates_ref, slots_ref,
    att_out, lay_out,
    qb, kv, wb, gub, db, res, heads, part, relay, plus, minus, att, place, comb_hi, comb_lo, gain_b,
    disp, xr, xall, acc, hid, ypart, relay2, plus2, minus2, yb, eb,
    ssem, rsem, lsem, ready,
):
    ctx = lax.axis_index("ctx")
    ex = lax.axis_index("exp")
    z, c = ctx // 2, ctx % 2
    x, y = ex // 4, ex % 4

    def at_z(d):
        return (lax.rem(z + d + NZ, NZ) * 2 + c, ex)

    def at_x(d):
        return (ctx, lax.rem(x + d + 4, 4) * 4 + y)

    def at_y(d):
        return (ctx, x * 4 + lax.rem(y + d + 4, 4))

    def at_xy(n, sign=1):
        return (ctx, lax.rem(x + sign * (n // 4) + 4, 4) * 4 + lax.rem(y + sign * (n % 4) + 4, 4))

    plane = sorted(range(1, BLOCKS), key=lambda n: -min(n // 4, 4 - n // 4) - min(n % 4, 4 - n % 4))

    other = (z * 2 + 1 - c, ex)

    barrier = pltpu.get_barrier_semaphore()
    peers = [other] + [at(d) for at in (at_z, at_x, at_y) for d in (1, 2, 3)]
    for peer in peers:
        pl.semaphore_signal(barrier, inc=1, device_id=peer, device_id_type=MESH)

    def local(src, dst, n):
        return pltpu.make_async_copy(src, dst, lsem.at[n])

    sent = []

    def remote(src, dst, n, dev):
        return pltpu.make_async_remote_copy(
            src_ref=src, dst_ref=dst, send_sem=ssem.at[n], recv_sem=rsem.at[n],
            device_id=dev, device_id_type=MESH,
        )

    def send(src, dst, n, dev):
        copy = remote(src, dst, n, dev)
        copy.start()
        sent.append(copy)
        return copy

    my_head = (z // 2) * HD
    mine = (2 * z + c) * TOK
    my_rows = pl.ds(pl.multiple_of(mine, TOK), TOK)
    own_k = local(k_in.at[:, pl.ds(pl.multiple_of(my_head, HD), HD)], kv.at[my_rows, pl.ds(0, HD)], L_K)
    own_v = local(v_in.at[:, pl.ds(pl.multiple_of(my_head, HD), HD)], kv.at[my_rows, pl.ds(HD, HD)], L_V)
    own_q = local(q_in.at[:, pl.ds(pl.multiple_of(z * HW, HW), HW)], qb.at[0], L_Q)
    w_rows = pl.ds(pl.multiple_of(c * K_DEV, K_DEV), K_DEV)
    own_w = local(w_in, wb.at[w_rows], L_W)
    g_rows = pl.ds(pl.multiple_of(c * FF_DEV, FF_DEV), FF_DEV)
    u_rows = pl.ds(pl.multiple_of(FF_CHIP + c * FF_DEV, FF_DEV), FF_DEV)
    own_g = local(g_in, gub.at[g_rows], L_G)
    own_u = local(u_in, gub.at[u_rows], L_U)
    own_d = local(d_in, db.at[g_rows], L_D)
    own_res = local(res_in, res, L_RES)
    for copy in (own_k, own_v, own_q, own_w, own_res, own_g, own_u, own_d):
        copy.start()

    pl.semaphore_wait(barrier, len(peers))
    for d in (1, 2, 3):
        pl.semaphore_signal(ready, inc=1, device_id=at_x(d), device_id_type=MESH)

    kv_copies = {}
    for d in (2, 1, 3):
        head = (lax.rem(z + d, NZ) // 2) * HD
        lanes = pl.ds(pl.multiple_of(head, HD), HD)
        kv_copies[d] = (
            send(k_in.at[:, lanes], kv.at[my_rows, pl.ds(0, HD)], S_KV + 2 * d, at_z(d)),
            send(v_in.at[:, lanes], kv.at[my_rows, pl.ds(HD, HD)], S_KV + 2 * d + 1, at_z(d)),
        )
    def q_send(d):
        lanes = pl.ds(pl.multiple_of(lax.rem(z + d, NZ) * HW, HW), HW)
        return send(q_in.at[:, lanes], qb.at[d], S_Q + d, at_z(d))

    q_send(2)
    w_copy = send(w_in, wb.at[w_rows], S_W, other)

    kv[:, pl.ds(2 * HD, HD)] = jnp.ones((SEQ, HD), BF16)
    ids = ids_ref[...]
    slots = slots_ref[...]
    gates = gates_ref[...]
    dest = ((ids // 4 - x) & 3) * 64 + (((ids & 3) - y) & 3) * 16 + slots
    dest = jnp.where(slots >= 0, dest, -16)
    row = lax.broadcasted_iota(jnp.int32, (STACK, TOK), 0)
    for quarter in range(4):
        placing = jnp.zeros((STACK, TOK), F32)
        combine = jnp.zeros((STACK, TOK), F32)
        for k in range(8):
            hit = row == dest[k : k + 1] + 4 * quarter
            placing += jnp.where(hit, 1.0, 0.0)
            combine += jnp.where(hit, gates[k : k + 1], 0.0)
        place[quarter] = placing.astype(BF16)
        combine = combine.T
        high = combine.astype(BF16)
        comb_hi[quarter] = high
        comb_lo[quarter] = (combine - high.astype(F32)).astype(BF16)
    gain_b[...] = jnp.broadcast_to(gain_ref[...], (8, D))

    own_k.wait()
    own_v.wait()
    kv_lanes = pl.ds(0, 2 * HD)
    fwd = [send(kv.at[my_rows, kv_lanes], kv.at[my_rows, kv_lanes], S_FWD, other)]
    for d in (1, 3, 2):
        kv_copies[d][0].wait_recv()
        kv_copies[d][1].wait_recv()
        rows = pl.ds(pl.multiple_of((lax.rem(z - d + NZ, NZ) * 2 + c) * TOK, TOK), TOK)
        fwd.append(send(kv.at[rows, kv_lanes], kv.at[rows, kv_lanes], S_FWD + d, other))
    q_send(1)
    q_send(3)
    ew_copies = (
        send(g_in, gub.at[g_rows], S_EW, other),
        send(u_in, gub.at[u_rows], S_EW + 1, other),
        send(d_in, db.at[g_rows], S_EW + 2, other),
    )
    for copy in fwd:
        copy.wait_recv()

    scale = HD**-0.5

    def attend(d, owner):
        limit = c * TOK + lax.broadcasted_iota(jnp.int32, (TOK, 2 * TOK), 0)
        seen = lax.broadcasted_iota(jnp.int32, (TOK, 2 * TOK), 1) <= limit
        for v in range(NZ):

            @pl.when(owner == v)
            def _():
                keys = kv[pl.ds(0, 2 * TOK * (v + 1)), pl.ds(0, HD)]
                vals = kv[pl.ds(0, 2 * TOK * (v + 1)), pl.ds(HD, 2 * HD)]
                for h in range(HEADS):
                    lanes = pl.ds(h * HD, HD)
                    s = lax.dot_general(qb[d, :, lanes], keys, NT, preferred_element_type=F32)
                    tail = jnp.where(seen, s[:, 2 * TOK * v :], -jnp.inf)
                    s = tail if v == 0 else jnp.concatenate([s[:, : 2 * TOK * v], tail], axis=1)
                    top = jnp.max(s, axis=1, keepdims=True)
                    p = jnp.exp((s - top) * scale).astype(BF16)
                    o = jnp.dot(p, vals, preferred_element_type=F32)
                    heads[:, lanes] = (o[:, :HD] / o[:, HD:]).astype(BF16)

    def relay_copy(src, dst, base, j):
        return remote(src, dst, base + j, at_z(1 if j % 2 == 0 else -1))

    def p_relay1(j):
        return relay_copy(part.at[2, :, cols(j)], relay.at[:, cols(j)], S_RELAY1, j)

    def p_plus1(j):
        return remote(part.at[1, :, cols(j)], plus.at[:, cols(j)], S_PLUS1 + j, at_z(-1))

    def p_minus1(j):
        return remote(part.at[3, :, cols(j)], minus.at[:, cols(j)], S_MINUS1 + j, at_z(1))

    def step_body(step, _):
        d = jnp.where(step == 0, 2, jnp.where(step == 1, 1, jnp.where(step == 2, 3, 0)))
        owner = lax.rem(z - d + NZ, NZ)

        @pl.when(step < 3)
        def _():
            pltpu.make_async_copy(qb.at[0], qb.at[d], rsem.at[S_Q + d]).wait()

        @pl.when(step == 3)
        def _():
            own_q.wait()

        attend(d, owner)

        @pl.when(step == 0)
        def _():
            own_w.wait()
            w_copy.wait_recv()

        for j in range(NCH):
            part[d, :, cols(j)] = jnp.dot(heads[...], wb[:, cols(j)], preferred_element_type=F32).astype(BF16)

            @pl.when(step == 0)
            def _():
                p_relay1(j).start()

            if j == 0:

                @pl.when(step == 1)
                def _():
                    p_plus1(j).start()

            if j == 1:

                @pl.when(step == 2)
                def _():
                    p_minus1(j).start()

        return 0

    lax.fori_loop(0, 4, step_body, 0)

    for j in range(NCH):
        joined, copy, direct = (3, p_minus1, p_plus1) if j % 2 == 0 else (1, p_plus1, p_minus1)
        p_relay1(j).wait_recv()
        part[joined, :, cols(j)] = (
            part[joined, :, cols(j)].astype(F32) + relay[:, cols(j)].astype(F32)
        ).astype(BF16)
        copy(j).start()
        if j >= 2:
            direct(j).start()
        sent.extend([p_relay1(j), p_plus1(j), p_minus1(j)])

    def pick(quarter, stacked_axis):
        shape = (ROWS, STACK) if stacked_axis else (STACK, ROWS)
        at = lax.broadcasted_iota(jnp.int32, shape, stacked_axis)
        slot_row = lax.broadcasted_iota(jnp.int32, shape, 1 - stacked_axis)
        return jnp.where(at == (slot_row // 4) * 16 + 4 * quarter + slot_row % 4, 1.0, 0.0).astype(BF16)

    own_res.wait()
    pl.semaphore_wait(ready, 3)
    square = jnp.zeros((TOK, 1), F32)
    own_copies = []

    def out_copy(p, n):
        rows = pl.ds(16 * n, 16)
        return remote(disp.at[rows, qcols(p)], xr.at[rows, qcols(p)], S_OUT + BLOCKS * p + n, at_xy(n))

    def g1(j):
        return remote(xall.at[pl.ds(0, ROWS), xcols(j)], xall.at[pl.ds(ROWS, ROWS), xcols(j)], S_G1 + j, at_z(1))

    def g3(j):
        return remote(xall.at[pl.ds(0, ROWS), xcols(j)], xall.at[pl.ds(3 * ROWS, ROWS), xcols(j)], S_G3 + j, at_z(-1))

    def g2(j):
        slot, way = (1, 1) if j % 2 == 0 else (3, -1)
        return remote(
            xall.at[pl.ds(slot * ROWS, ROWS), xcols(j)], xall.at[pl.ds(2 * ROWS, ROWS), xcols(j)], S_G2 + j, at_z(way)
        )

    def start(copies):
        for copy in copies:
            copy.start()
            sent.append(copy)

    def attended_chunk(j, square):
        p_plus1(j).wait_recv()
        p_minus1(j).wait_recv()
        total = (
            part[0, :, cols(j)].astype(F32) + plus[:, cols(j)].astype(F32) + minus[:, cols(j)].astype(F32)
        )
        a = (res[:, cols(j)].astype(F32) + total).astype(BF16)
        att[:, cols(j)] = a
        copy = local(att.at[:, cols(j)], att_out.at[:, cols(j)], L_ATT + j)
        copy.start()
        own_copies.append(copy)
        a = a.astype(F32)
        square += jnp.sum(a * a, axis=1, keepdims=True)
        scaled = (a * gain_b[pl.ds(0, 1), cols(j)]).astype(BF16)
        return square, scaled

    def dispatch_half(p, square):
        stack = jnp.zeros((STACK, QW), F32)
        for j in (2 * p, 2 * p + 1):
            square, scaled = attended_chunk(j, square)
            for i in range(2):
                stack += jnp.dot(place[2 * (j % 2) + i], scaled[:, i * QW : (i + 1) * QW], preferred_element_type=F32)
        stack = stack.astype(BF16)
        disp[:, pl.ds(p * QW, QW)] = stack
        xr[pl.ds(0, 16), pl.ds(p * QW, QW)] = stack[:16]
        if p == 1:
            norm = lax.rsqrt(square * (1.0 / D) + 1e-06)
            norm = jnp.broadcast_to(norm, (TOK, SCALE_COLS))
            norm_hi = norm.astype(BF16).astype(F32)
            lane = lax.broadcasted_iota(jnp.int32, (TOK, SCALE_COLS), 1)
            both = jnp.where(lane < SCALE_COLS // 2, norm_hi, norm - norm_hi).astype(BF16)
            stack = jnp.dot(place[0], both, preferred_element_type=F32).astype(BF16)
            disp[:, pl.ds(2 * QW, SCALE_COLS)] = stack
            xr[pl.ds(0, 16), pl.ds(2 * QW, SCALE_COLS)] = stack[:16]
        start([out_copy(p, n) for n in plane])
        return square

    def gather_half(p):
        for n in plane:
            out_copy(p, n).wait_recv()
        stack = xr[:, pl.ds(p * QW, QW)]
        for quarter in range(4):
            rows = jnp.dot(pick(quarter, 1), stack, preferred_element_type=F32).astype(BF16)
            xall[pl.ds(0, ROWS), pl.ds(p * HALF + quarter * QW, QW)] = rows
        if p == 1:
            rows = jnp.dot(pick(0, 1), xr[:, pl.ds(2 * QW, SCALE_COLS)], preferred_element_type=F32).astype(BF16)
            xall[pl.ds(0, ROWS), pl.ds(D, SCALE_COLS)] = rows
        for j in (2 * p, 2 * p + 1):
            start([g1(j), g3(j)])

    def pass_chunk(j):
        (g1(j) if j % 2 == 0 else g3(j)).wait_recv()
        start([g2(j)])

    def gate_up_chunk(j):
        (g3(j) if j % 2 == 0 else g1(j)).wait_recv()
        g2(j).wait_recv()
        prod = lax.dot_general(xall[:, cols(j)], gub[:, cols(j)], NT, preferred_element_type=F32)
        acc[...] = prod if j == 0 else acc[...] + prod

    square = dispatch_half(0, square)
    gather_half(0)
    square = dispatch_half(1, square)
    for j in (0, 1):
        pass_chunk(j)
    gather_half(1)
    own_g.wait()
    own_u.wait()
    own_d.wait()
    for copy in ew_copies:
        copy.wait_recv()
    for j in (0, 1):
        gate_up_chunk(j)
    for j in (2, 3):
        pass_chunk(j)
    for j in (2, 3):
        gate_up_chunk(j)

    sc = xall[:, pl.ds(D, SCALE_COLS)].astype(F32)
    sc = sc[:, 0:1] + sc[:, SCALE_COLS // 2 : SCALE_COLS // 2 + 1]
    gate = acc[:, pl.ds(0, FF_CHIP)] * sc
    upper = acc[:, pl.ds(FF_CHIP, FF_CHIP)] * sc
    hid[...] = (gate * jax.nn.sigmoid(gate) * upper).astype(BF16)

    def q_relay2(j):
        return relay_copy(ypart.at[pl.ds(2 * ROWS, ROWS), cols(j)], relay2.at[:, cols(j)], S_RELAY2, j)

    def q_plus2(j):
        return remote(ypart.at[pl.ds(ROWS, ROWS), cols(j)], plus2.at[:, cols(j)], S_PLUS2 + j, at_z(-1))

    def q_minus2(j):
        return remote(ypart.at[pl.ds(3 * ROWS, ROWS), cols(j)], minus2.at[:, cols(j)], S_MINUS2 + j, at_z(1))

    for j in range(NCH):
        ypart[:, cols(j)] = jnp.dot(hid[...], db[:, cols(j)], preferred_element_type=F32).astype(BF16)
        start([q_relay2(j)])
    start([q_plus2(0), q_minus2(1)])
    for j in range(NCH):
        joined, copy, direct = (3, q_minus2, q_plus2) if j % 2 == 0 else (1, q_plus2, q_minus2)
        q_relay2(j).wait_recv()
        rows = pl.ds(joined * ROWS, ROWS)
        ypart[rows, cols(j)] = (ypart[rows, cols(j)].astype(F32) + relay2[:, cols(j)].astype(F32)).astype(BF16)
        start([copy(j)])
        if j >= 2:
            start([direct(j)])

    def back_copy(p, n):
        rows = pl.ds(16 * n, 16)
        lanes = pl.ds(p * QW, QW)
        return remote(yb.at[rows, lanes], eb.at[rows, lanes], S_BACK + BLOCKS * p + n, at_xy(n, -1))

    def return_half(p):
        stack = jnp.zeros((STACK, QW), F32)
        for j in (2 * p, 2 * p + 1):
            q_plus2(j).wait_recv()
            q_minus2(j).wait_recv()
            rows = (
                ypart[pl.ds(0, ROWS), cols(j)].astype(F32)
                + plus2[:, cols(j)].astype(F32)
                + minus2[:, cols(j)].astype(F32)
            ).astype(BF16)
            for i in range(2):
                stack += jnp.dot(pick(2 * (j % 2) + i, 0), rows[:, i * QW : (i + 1) * QW], preferred_element_type=F32)
        stack = stack.astype(BF16)
        yb[:, pl.ds(p * QW, QW)] = stack
        eb[pl.ds(0, 16), pl.ds(p * QW, QW)] = stack[:16]
        start([back_copy(p, n) for n in plane])

    def combine_half(p):
        for n in plane:
            back_copy(p, n).wait_recv()
        stack = eb[:, pl.ds(p * QW, QW)]
        for quarter in range(4):
            lanes = pl.ds(p * HALF + quarter * QW, QW)
            moe = jnp.dot(comb_hi[quarter], stack, preferred_element_type=F32)
            moe += jnp.dot(comb_lo[quarter], stack, preferred_element_type=F32)
            plus[:, lanes] = (att[:, lanes].astype(F32) + moe).astype(BF16)
        lanes = pl.ds(p * HALF, HALF)
        copy = local(plus.at[:, lanes], lay_out.at[:, lanes], L_OUT + p)
        copy.start()
        own_copies.append(copy)

    return_half(0)
    combine_half(0)
    return_half(1)
    combine_half(1)

    for copy in own_copies:
        copy.wait()
    for copy in sent:
        copy.wait_send()


def shards(
    queries, keys, values, residual, out_weight, norm_gain, expert_ids, gate_weights, slots, w_gate, w_up, w_down
):
    out = jax.ShapeDtypeStruct((TOK, D), BF16)
    hbm = pl.BlockSpec(memory_space=pl.ANY)
    vmem = pl.BlockSpec(memory_space=pltpu.VMEM)

    def buf(*shape, dtype=BF16):
        return pltpu.VMEM(shape, dtype)

    attended, layer_out = pl.pallas_call(
        layer,
        out_shape=(out, out),
        in_specs=[hbm] * 8 + [vmem] * 4,
        out_specs=(hbm, hbm),
        scratch_shapes=[
            buf(NZ, TOK, HW),
            buf(SEQ, 3 * HD),
            buf(2 * K_DEV, D),
            buf(2 * FF_CHIP, D),
            buf(FF_CHIP, D),
            buf(TOK, D),
            buf(TOK, HW),
            buf(NZ, TOK, D),
            buf(TOK, D),
            buf(TOK, D),
            buf(TOK, D),
            buf(TOK, D),
            buf(4, STACK, TOK),
            buf(4, TOK, STACK),
            buf(4, TOK, STACK),
            buf(8, D, dtype=F32),
            buf(STACK, 2 * QW + SCALE_COLS),
            buf(STACK, 2 * QW + SCALE_COLS),
            buf(NZ * ROWS, DX),
            buf(NZ * ROWS, 2 * FF_CHIP, dtype=F32),
            buf(NZ * ROWS, FF_CHIP),
            buf(NZ * ROWS, D),
            buf(ROWS, D),
            buf(ROWS, D),
            buf(ROWS, D),
            buf(STACK, 2 * QW),
            buf(STACK, 2 * QW),
            pltpu.SemaphoreType.DMA((N_SEM,)),
            pltpu.SemaphoreType.DMA((N_SEM,)),
            pltpu.SemaphoreType.DMA((N_LOC,)),
            pltpu.SemaphoreType.REGULAR,
        ],
        compiler_params=pltpu.CompilerParams(collective_id=0, has_side_effects=True, vmem_limit_bytes=56 << 20),
        name="decoder_layer",
    )(
        queries[0], keys[0], values[0], residual[0], out_weight,
        w_gate[0].T, w_up[0].T, w_down[0], norm_gain[None],
        expert_ids[0].T, gate_weights[0].T, slots[0].T,
    )
    return attended[None], layer_out[None]


def solution(mesh):
    rows = P("exp", "ctx", None)
    placed = (rows, rows, rows, rows, P("ctx", None), P(), rows, rows, rows,
              P("exp", None, "ctx"), P("exp", None, "ctx"), rows)
    return jax.shard_map(shards, mesh=mesh, in_specs=placed, out_specs=(rows, rows), check_vma=False)
```

```python
import functools

import jax
import jax.numpy as jnp
from jax import lax
from jax.experimental import pallas as pl
from jax.experimental.pallas import tpu as pltpu
from jax.sharding import PartitionSpec as P

D = 4096
HD = 128
QH = 32
TOK = 128
NZ = 4
HEADS = QH // NZ
HW = HEADS * HD
SEQ = 1024
FF_DEV = 192
FF_CHIP = 2 * FF_DEV
K_DEV = 512
CAP = 4
ROWS = 64
SCALE_COLS = 128
NCH = 4
CW = D // NCH
DX = D + SCALE_COLS
HALF = D // 2
QW = HALF // 4
BLOCKS = 16
STACK = 4 * ROWS
F32 = jnp.float32
BF16 = jnp.bfloat16
MESH = pl.DeviceIdType.MESH

NT = (((1,), (1,)), ((), ()))


def cols(j):
    return pl.ds(j * CW, CW)


def xcols(j):
    return pl.ds(j * CW, CW + (SCALE_COLS if j == NCH - 1 else 0))


def qcols(p):
    return pl.ds(p * QW, QW + (SCALE_COLS if p == 1 else 0))


_count = 0


def _take(n):
    global _count
    first = _count
    _count += n
    return first


S_Q = _take(7)
S_KV = _take(16)
S_FWD = _take(4)
S_W = _take(1)
S_EW = _take(3)
S_WZ = _take(4)
S_W1 = _take(16)
S_W2 = _take(16)
S_W3 = _take(16)
S_WF = _take(16)
S_P = _take(8)
S_OUT = _take(2 * BLOCKS)
S_G1 = _take(NCH)
S_G2 = _take(NCH)
S_G3 = _take(NCH)
S_RELAY2 = _take(NCH)
S_PLUS2 = _take(NCH)
S_MINUS2 = _take(NCH)
S_BACK = _take(2 * BLOCKS)
N_SEM = _count

L_Q = 0
L_KV = 3
L_W = 7
L_G = 8
L_U = 9
L_D = 10
L_RES = 11
L_ATT = 12
L_OUT = L_ATT + NCH
N_LOC = L_OUT + NCH


def layer(
    q_in, k_in, v_in, res_in, w_in, g_in, u_in, d_in, gain_ref, ids_ref, gates_ref, slots_ref,
    both_out,
    qb, kv, wb, wa_part, wb_part, gub, db, res, heads, proj, send_a, send_b, recv_a, recv_b, att, lay,
    place, comb_hi, comb_lo, gain_b,
    disp, xr, xall, acc, hid, ypart, relay2, plus2, minus2, yb, eb,
    ssem, rsem, lsem, ready,
):
    ctx = lax.axis_index("ctx")
    ex = lax.axis_index("exp")
    z, c = ctx // 2, ctx % 2
    x, y = ex // 4, ex % 4

    za, zb, zc = z + 1 - 2 * lax.rem(z, 2), NZ - 1 - z, lax.rem(z + 2, NZ)
    dev_a, dev_b = (za * 2 + c, ex), (zb * 2 + c, ex)

    def at_z(d):
        return (lax.rem(z + d + NZ, NZ) * 2 + c, ex)

    def at_x(d):
        return (ctx, lax.rem(x + d + 4, 4) * 4 + y)

    def at_y(d):
        return (ctx, x * 4 + lax.rem(y + d + 4, 4))

    def at_xy(n, sign=1):
        return (ctx, lax.rem(x + sign * (n // 4) + 4, 4) * 4 + lax.rem(y + sign * (n % 4) + 4, 4))

    plane = sorted(range(1, BLOCKS), key=lambda n: -min(n // 4, 4 - n // 4) - min(n % 4, 4 - n % 4))

    other = (z * 2 + 1 - c, ex)

    barrier = pltpu.get_barrier_semaphore()
    peers = [other] + [at(d) for at in (at_z, at_x, at_y) for d in (1, 2, 3)]
    for peer in peers:
        pl.semaphore_signal(barrier, inc=1, device_id=peer, device_id_type=MESH)

    def local(src, dst, n):
        return pltpu.make_async_copy(src, dst, lsem.at[n])

    sent = []

    def remote(src, dst, n, dev):
        return pltpu.make_async_remote_copy(
            src_ref=src, dst_ref=dst, send_sem=ssem.at[n], recv_sem=rsem.at[n],
            device_id=dev, device_id_type=MESH,
        )

    def send(src, dst, n, dev):
        copy = remote(src, dst, n, dev)
        copy.start()
        sent.append(copy)
        return copy

    mine = (2 * z + c) * TOK
    my_rows = pl.ds(pl.multiple_of(mine, TOK), TOK)

    def kv_parts():
        for h in range(2):
            for i, src in enumerate((k_in, v_in)):
                yield 2 * h + i, src.at[:, pl.ds(h * HD, HD)], kv.at[h, my_rows, pl.ds(i * HD, HD)]

    own_kv = [local(src, dst, L_KV + n) for n, src, dst in kv_parts()]

    def q_lanes(group):
        return q_in.at[:, pl.ds(pl.multiple_of(group * HW, HW), HW)]

    own_q = [local(q_lanes(g), qb.at[slot], L_Q + i) for i, (slot, g) in enumerate(((1, z), (4, za), (5, zb)))]
    w_rows = pl.ds(pl.multiple_of(c * K_DEV, K_DEV), K_DEV)
    own_w = local(w_in, wb.at[w_rows], L_W)
    g_rows = pl.ds(pl.multiple_of(c * FF_DEV, FF_DEV), FF_DEV)
    u_rows = pl.ds(pl.multiple_of(FF_CHIP + c * FF_DEV, FF_DEV), FF_DEV)
    own_g = local(g_in, gub.at[g_rows], L_G)
    own_u = local(u_in, gub.at[u_rows], L_U)
    own_d = local(d_in, db.at[g_rows], L_D)
    own_res = local(res_in, res, L_RES)
    for copy in (*own_kv, *own_q, own_w, own_res, own_g, own_u, own_d):
        copy.start()

    pl.semaphore_wait(barrier, len(peers))
    for d in (1, 2, 3):
        pl.semaphore_signal(ready, inc=1, device_id=at_x(d), device_id_type=MESH)

    row0 = c * K_DEV

    def w_part(buf, first, count, rnd, lane=0, lanes=CW):
        return buf.at[pl.ds(pl.multiple_of(row0 + first, 32), count), pl.ds(rnd * CW + lane, lanes)]

    ways = (
        (wa_part, 0, dev_a, 4 * x + y, x, at_y, at_x),
        (wb_part, D // 2, dev_b, 4 * y + x, y, at_x, at_y),
    )

    def w_step0(rnd):
        for i, (buf, lane, dev, piece, _, _, _) in enumerate(ways):
            first = pl.multiple_of(32 * piece, 32)
            src = w_in.at[pl.ds(first, 32), pl.ds(lane + rnd * CW, CW)]
            yield remote(src, w_part(buf, first, 32, rnd), S_WZ + 2 * rnd + i, dev)

    def w_step1(rnd):
        for i, (buf, _, _, piece, _, at1, _) in enumerate(ways):
            for d in (2, 1, 3):
                ref = w_part(buf, 32 * piece, 32, rnd)
                yield remote(ref, ref, S_W1 + 8 * rnd + 4 * i + d, at1(d))

    def w_step2(rnd):
        for i, (buf, _, _, _, block, _, at2) in enumerate(ways):
            for d in (1, 3):
                ref = w_part(buf, 128 * block, 128, rnd)
                yield remote(ref, ref, S_W2 + 8 * rnd + 4 * i + d, at2(d))

    def w_step3(rnd):
        for i, (buf, _, _, _, block, _, at2) in enumerate(ways):
            for d in (1, 3):
                ref = w_part(buf, 128 * lax.rem(block + 4 - d, 4), 128, rnd, (d // 2) * (CW // 2), CW // 2)
                yield remote(ref, ref, S_W3 + 8 * rnd + 4 * i + d, at2(d))

    def w_swap(rnd, which):
        for i, (buf, _, _, _, block, _, _) in enumerate(ways):
            for d in which:
                ref = w_part(buf, 128 * lax.rem(block + 4 - d, 4), 128, rnd)
                yield remote(ref, ref, S_WF + 8 * rnd + 4 * i + d, other)

    def begin(copies):
        for copy in copies:
            copy.start()

    def arrive(copies):
        for copy in copies:
            copy.wait_recv()

    begin(w_step0(0))
    kv_copies = {
        d: [send(src, dst, S_KV + 4 * d + n, at_z(d)) for n, src, dst in kv_parts()] for d in (2, 1, 3)
    }
    begin(w_step0(1))
    q_copies = [
        send(q_lanes(group), qb.at[slot], S_Q + slot, dev)
        for slot, group, dev in ((0, zb, dev_b), (2, za, dev_a), (3, zc, dev_b), (6, zc, dev_a))
    ]
    w_copy = send(w_in, wb.at[w_rows], S_W, other)

    for h in range(2):
        kv[h, :, pl.ds(2 * HD, HD)] = jnp.ones((SEQ, HD), BF16)
    ids = ids_ref[...]
    slots = slots_ref[...]
    gates = gates_ref[...]
    dest = ((ids // 4 - x) & 3) * 64 + (((ids & 3) - y) & 3) * 16 + slots
    dest = jnp.where(slots >= 0, dest, -16)
    row = lax.broadcasted_iota(jnp.int32, (STACK, TOK), 0)
    for quarter in range(4):
        placing = jnp.zeros((STACK, TOK), F32)
        combine = jnp.zeros((STACK, TOK), F32)
        for k in range(8):
            hit = row == dest[k : k + 1] + 4 * quarter
            placing += jnp.where(hit, 1.0, 0.0)
            combine += jnp.where(hit, gates[k : k + 1], 0.0)
        place[quarter] = placing.astype(BF16)
        combine = combine.T
        high = combine.astype(BF16)
        comb_hi[quarter] = high
        comb_lo[quarter] = (combine - high.astype(F32)).astype(BF16)
    gain_b[...] = jnp.broadcast_to(gain_ref[...], (8, D))

    for copy in own_kv:
        copy.wait()
    kv_lanes = pl.ds(0, 2 * HD)
    fwd = [send(kv.at[:, my_rows, kv_lanes], kv.at[:, my_rows, kv_lanes], S_FWD, other)]
    arrive(w_step0(0))
    begin(w_step1(0))
    for d in (1, 3, 2):
        arrive(kv_copies[d])
        rows = pl.ds(pl.multiple_of((lax.rem(z - d + NZ, NZ) * 2 + c) * TOK, TOK), TOK)
        fwd.append(send(kv.at[:, rows, kv_lanes], kv.at[:, rows, kv_lanes], S_FWD + d, other))
    arrive(w_step0(1))
    begin(w_step1(1))
    arrive(w_step1(0))
    begin(w_step2(0))
    begin(w_swap(0, (0,)))
    ew_copies = (
        send(g_in, gub.at[g_rows], S_EW, other),
        send(u_in, gub.at[u_rows], S_EW + 1, other),
        send(d_in, db.at[g_rows], S_EW + 2, other),
    )
    arrive(fwd)

    scale = HD**-0.5

    def attend(slot, owner, head):
        limit = c * TOK + lax.broadcasted_iota(jnp.int32, (TOK, 2 * TOK), 0)
        seen = lax.broadcasted_iota(jnp.int32, (TOK, 2 * TOK), 1) <= limit
        for v in range(NZ):

            @pl.when(owner == v)
            def _():
                keys = kv[head, pl.ds(0, 2 * TOK * (v + 1)), pl.ds(0, HD)]
                vals = kv[head, pl.ds(0, 2 * TOK * (v + 1)), pl.ds(HD, 2 * HD)]
                for h in range(HEADS):
                    lanes = pl.ds(h * HD, HD)
                    s = lax.dot_general(qb[slot, :, lanes], keys, NT, preferred_element_type=F32)
                    tail = jnp.where(seen, s[:, 2 * TOK * v :], -jnp.inf)
                    s = tail if v == 0 else jnp.concatenate([s[:, : 2 * TOK * v], tail], axis=1)
                    top = jnp.max(s, axis=1, keepdims=True)
                    p = jnp.exp((s - top) * scale).astype(BF16)
                    o = jnp.dot(p, vals, preferred_element_type=F32)
                    heads[pl.ds(pl.multiple_of(slot * TOK, TOK), TOK), lanes] = (o[:, :HD] / o[:, HD:]).astype(BF16)

    order = (1, 4, 5, 0, 2, 3, 6)
    owners = (zb, z, za, zb, z, z, za)
    groups = (z, z, z, za, za, zb, zb)

    def choose(step, values):
        out = values[order[0]]
        for n in range(1, 7):
            out = jnp.where(step == n, values[order[n]], out)
        return out

    for copy in own_q:
        copy.wait()

    def step_body(step, _):
        slot = choose(step, tuple(range(7)))

        @pl.when(step >= 3)
        def _():
            pltpu.make_async_copy(qb.at[1], qb.at[slot], rsem.at[S_Q + slot]).wait()

        attend(slot, choose(step, owners), choose(step, groups) // 2)

        @pl.when(step == 2)
        def _():
            arrive(w_step2(0))
            begin(w_step3(0))
            begin(w_swap(0, (1, 3)))
            arrive(w_step1(1))
            begin(w_step2(1))
            begin(w_swap(1, (0,)))

        return 0

    lax.fori_loop(0, 7, step_body, 0)

    def p_a(j, i):
        lanes = pl.ds(j * CW + i * QW, QW)
        return remote(send_a.at[:, lanes], recv_a.at[:, lanes], S_P + 2 * j + i, dev_b)

    def p_b(j, i):
        lanes = pl.ds((j - 2) * CW + i * QW, QW)
        return remote(send_b.at[:, lanes], recv_b.at[:, lanes], S_P + 2 * j + i, dev_a)

    def project(rnd):
        for i in range(2):
            lanes = pl.ds(rnd * CW + i * QW, QW)
            out = jnp.dot(heads[pl.ds(0, 2 * TOK), :], wb[:, lanes], preferred_element_type=F32)
            out += jnp.dot(heads[pl.ds(3 * TOK, 2 * TOK), :], wa_part[:, lanes], preferred_element_type=F32)
            send_a[:, lanes] = out[:TOK].astype(BF16)
            p_a(rnd, i).start()
            proj[:, lanes] = out[TOK:]
            wide = pl.ds(D // 2 + rnd * CW + i * QW, QW)
            out = jnp.dot(heads[pl.ds(TOK, 2 * TOK), :], wb[:, wide], preferred_element_type=F32)
            out += jnp.dot(heads[pl.ds(5 * TOK, 2 * TOK), :], wb_part[:, lanes], preferred_element_type=F32)
            send_b[:, lanes] = out[TOK:].astype(BF16)
            p_b(2 + rnd, i).start()
            proj[:, wide] = out[:TOK]
            sent.extend([p_a(rnd, i), p_b(2 + rnd, i)])

    def pick(quarter, stacked_axis):
        shape = (ROWS, STACK) if stacked_axis else (STACK, ROWS)
        at = lax.broadcasted_iota(jnp.int32, shape, stacked_axis)
        slot_row = lax.broadcasted_iota(jnp.int32, shape, 1 - stacked_axis)
        return jnp.where(at == (slot_row // 4) * 16 + 4 * quarter + slot_row % 4, 1.0, 0.0).astype(BF16)

    own_res.wait()
    pl.semaphore_wait(ready, 3)
    square = jnp.zeros((TOK, 1), F32)
    own_copies = []

    def out_copy(p, n):
        rows = pl.ds(16 * n, 16)
        return remote(disp.at[rows, qcols(p)], xr.at[rows, qcols(p)], S_OUT + BLOCKS * p + n, at_xy(n))

    def g1(j):
        return remote(xall.at[pl.ds(0, ROWS), xcols(j)], xall.at[pl.ds(ROWS, ROWS), xcols(j)], S_G1 + j, at_z(1))

    def g3(j):
        return remote(xall.at[pl.ds(0, ROWS), xcols(j)], xall.at[pl.ds(3 * ROWS, ROWS), xcols(j)], S_G3 + j, at_z(-1))

    def g2(j):
        slot, way = (1, 1) if j < 2 else (3, -1)
        return remote(
            xall.at[pl.ds(slot * ROWS, ROWS), xcols(j)], xall.at[pl.ds(2 * ROWS, ROWS), xcols(j)], S_G2 + j, at_z(way)
        )

    def start(copies):
        for copy in copies:
            copy.start()
            sent.append(copy)

    def attended_chunk(j, square):
        for i in range(2):
            (p_a if j < 2 else p_b)(j, i).wait_recv()
        lanes = pl.ds((j % 2) * CW, CW)
        total = proj[:, cols(j)] + (recv_a if j < 2 else recv_b)[:, lanes].astype(F32)
        a = (res[:, cols(j)].astype(F32) + total).astype(BF16)
        att[:, cols(j)] = a
        copy = local(att.at[:, cols(j)], both_out.at[0, :, cols(j)], L_ATT + j)
        copy.start()
        own_copies.append(copy)
        a = a.astype(F32)
        square += jnp.sum(a * a, axis=1, keepdims=True)
        scaled = (a * gain_b[pl.ds(0, 1), cols(j)]).astype(BF16)
        return square, scaled

    def dispatch_half(p, square):
        stack = jnp.zeros((STACK, QW), F32)
        for j in (p, 2 + p):
            square, scaled = attended_chunk(j, square)
            for i in range(2):
                stack += jnp.dot(place[2 * (j // 2) + i], scaled[:, i * QW : (i + 1) * QW], preferred_element_type=F32)
        stack = stack.astype(BF16)
        disp[:, pl.ds(p * QW, QW)] = stack
        xr[pl.ds(0, 16), pl.ds(p * QW, QW)] = stack[:16]
        if p == 1:
            norm = lax.rsqrt(square * (1.0 / D) + 1e-06)
            norm = jnp.broadcast_to(norm, (TOK, SCALE_COLS))
            norm_hi = norm.astype(BF16).astype(F32)
            lane = lax.broadcasted_iota(jnp.int32, (TOK, SCALE_COLS), 1)
            both = jnp.where(lane < SCALE_COLS // 2, norm_hi, norm - norm_hi).astype(BF16)
            stack = jnp.dot(place[0], both, preferred_element_type=F32).astype(BF16)
            disp[:, pl.ds(2 * QW, SCALE_COLS)] = stack
            xr[pl.ds(0, 16), pl.ds(2 * QW, SCALE_COLS)] = stack[:16]
        start([out_copy(p, n) for n in plane])
        return square

    def gather_half(p):
        for n in plane:
            out_copy(p, n).wait_recv()
        stack = xr[:, pl.ds(p * QW, QW)]
        for quarter in range(4):
            rows = jnp.dot(pick(quarter, 1), stack, preferred_element_type=F32).astype(BF16)
            xall[pl.ds(0, ROWS), pl.ds((quarter // 2) * HALF + p * CW + (quarter % 2) * QW, QW)] = rows
        if p == 1:
            rows = jnp.dot(pick(0, 1), xr[:, pl.ds(2 * QW, SCALE_COLS)], preferred_element_type=F32).astype(BF16)
            xall[pl.ds(0, ROWS), pl.ds(D, SCALE_COLS)] = rows
        for j in (p, 2 + p):
            start([g1(j), g3(j)])

    def pass_chunk(j):
        (g1(j) if j < 2 else g3(j)).wait_recv()
        start([g2(j)])

    def gate_up_chunk(j):
        (g3(j) if j < 2 else g1(j)).wait_recv()
        g2(j).wait_recv()
        prod = lax.dot_general(xall[:, cols(j)], gub[:, cols(j)], NT, preferred_element_type=F32)
        acc[...] = prod if j == 0 else acc[...] + prod

    own_w.wait()
    w_copy.wait_recv()
    arrive(w_step3(0))
    begin(w_swap(0, (2,)))
    arrive(w_swap(0, (0, 1, 3, 2)))
    project(0)
    arrive(w_step2(1))
    begin(w_step3(1))
    begin(w_swap(1, (1, 3)))
    square = dispatch_half(0, square)
    arrive(w_step3(1))
    begin(w_swap(1, (2,)))
    arrive(w_swap(1, (0, 1, 3, 2)))
    project(1)
    for rnd in (0, 1):
        for copies in (w_step0(rnd), w_step1(rnd), w_step2(rnd), w_step3(rnd), w_swap(rnd, (0, 1, 2, 3))):
            sent.extend(copies)
    gather_half(0)
    square = dispatch_half(1, square)
    for j in (0, 2):
        pass_chunk(j)
    gather_half(1)
    own_g.wait()
    own_u.wait()
    own_d.wait()
    for copy in ew_copies:
        copy.wait_recv()
    for j in (0, 2):
        gate_up_chunk(j)
    for j in (1, 3):
        pass_chunk(j)
    for j in (1, 3):
        gate_up_chunk(j)

    sc = xall[:, pl.ds(D, SCALE_COLS)].astype(F32)
    sc = sc[:, 0:1] + sc[:, SCALE_COLS // 2 : SCALE_COLS // 2 + 1]
    gate = acc[:, pl.ds(0, FF_CHIP)] * sc
    upper = acc[:, pl.ds(FF_CHIP, FF_CHIP)] * sc
    hid[...] = (gate * jax.nn.sigmoid(gate) * upper).astype(BF16)

    def relay_copy(src, dst, base, j):
        return remote(src, dst, base + j, at_z(1 if j % 2 == 0 else -1))

    def q_relay2(j):
        return relay_copy(ypart.at[pl.ds(2 * ROWS, ROWS), cols(j)], relay2.at[:, cols(j)], S_RELAY2, j)

    def q_plus2(j):
        return remote(ypart.at[pl.ds(ROWS, ROWS), cols(j)], plus2.at[:, cols(j)], S_PLUS2 + j, at_z(-1))

    def q_minus2(j):
        return remote(ypart.at[pl.ds(3 * ROWS, ROWS), cols(j)], minus2.at[:, cols(j)], S_MINUS2 + j, at_z(1))

    for j in range(NCH):
        ypart[:, cols(j)] = jnp.dot(hid[...], db[:, cols(j)], preferred_element_type=F32).astype(BF16)
        start([q_relay2(j)])
    start([q_plus2(0), q_minus2(1)])
    for j in range(NCH):
        joined, copy, direct = (3, q_minus2, q_plus2) if j % 2 == 0 else (1, q_plus2, q_minus2)
        q_relay2(j).wait_recv()
        rows = pl.ds(joined * ROWS, ROWS)
        ypart[rows, cols(j)] = (ypart[rows, cols(j)].astype(F32) + relay2[:, cols(j)].astype(F32)).astype(BF16)
        start([copy(j)])
        if j >= 2:
            start([direct(j)])

    def back_copy(p, n):
        rows = pl.ds(16 * n, 16)
        lanes = pl.ds(p * QW, QW)
        return remote(yb.at[rows, lanes], eb.at[rows, lanes], S_BACK + BLOCKS * p + n, at_xy(n, -1))

    def return_half(p):
        stack = jnp.zeros((STACK, QW), F32)
        for j in (2 * p, 2 * p + 1):
            q_plus2(j).wait_recv()
            q_minus2(j).wait_recv()
            rows = (
                ypart[pl.ds(0, ROWS), cols(j)].astype(F32)
                + plus2[:, cols(j)].astype(F32)
                + minus2[:, cols(j)].astype(F32)
            ).astype(BF16)
            for i in range(2):
                stack += jnp.dot(pick(2 * (j % 2) + i, 0), rows[:, i * QW : (i + 1) * QW], preferred_element_type=F32)
        stack = stack.astype(BF16)
        yb[:, pl.ds(p * QW, QW)] = stack
        eb[pl.ds(0, 16), pl.ds(p * QW, QW)] = stack[:16]
        start([back_copy(p, n) for n in plane])

    def combine_half(p):
        for n in plane:
            back_copy(p, n).wait_recv()
        stack = eb[:, pl.ds(p * QW, QW)]
        for quarter in range(4):
            lanes = pl.ds(p * HALF + quarter * QW, QW)
            moe = jnp.dot(comb_hi[quarter], stack, preferred_element_type=F32)
            moe += jnp.dot(comb_lo[quarter], stack, preferred_element_type=F32)
            lay[:, lanes] = (att[:, lanes].astype(F32) + moe).astype(BF16)
        lanes = pl.ds(p * HALF, HALF)
        copy = local(lay.at[:, lanes], both_out.at[1, :, lanes], L_OUT + p)
        copy.start()
        own_copies.append(copy)

    return_half(0)
    combine_half(0)
    return_half(1)
    combine_half(1)

    for copy in own_copies:
        copy.wait()
    for copy in sent:
        copy.wait_send()


def shards(
    queries, keys, values, residual, out_weight, norm_gain, expert_ids, gate_weights, slots, w_gate, w_up, w_down
):
    out = jax.ShapeDtypeStruct((2, TOK, D), BF16)
    hbm = pl.BlockSpec(memory_space=pl.ANY)
    vmem = pl.BlockSpec(memory_space=pltpu.VMEM)

    def buf(*shape, dtype=BF16):
        return pltpu.VMEM(shape, dtype)

    both = pl.pallas_call(
        layer,
        out_shape=out,
        in_specs=[hbm] * 8 + [vmem] * 4,
        out_specs=hbm,
        scratch_shapes=[
            buf(7, TOK, HW),
            buf(2, SEQ, 3 * HD),
            buf(2 * K_DEV, D),
            buf(2 * K_DEV, D // 2),
            buf(2 * K_DEV, D // 2),
            buf(2 * FF_CHIP, D),
            buf(FF_CHIP, D),
            buf(TOK, D),
            buf(7 * TOK, HW),
            buf(TOK, D, dtype=F32),
            buf(TOK, D // 2),
            buf(TOK, D // 2),
            buf(TOK, D // 2),
            buf(TOK, D // 2),
            buf(TOK, D),
            buf(TOK, D),
            buf(4, STACK, TOK),
            buf(4, TOK, STACK),
            buf(4, TOK, STACK),
            buf(8, D, dtype=F32),
            buf(STACK, 2 * QW + SCALE_COLS),
            buf(STACK, 2 * QW + SCALE_COLS),
            buf(NZ * ROWS, DX),
            buf(NZ * ROWS, 2 * FF_CHIP, dtype=F32),
            buf(NZ * ROWS, FF_CHIP),
            buf(NZ * ROWS, D),
            buf(ROWS, D),
            buf(ROWS, D),
            buf(ROWS, D),
            buf(STACK, 2 * QW),
            buf(STACK, 2 * QW),
            pltpu.SemaphoreType.DMA((N_SEM,)),
            pltpu.SemaphoreType.DMA((N_SEM,)),
            pltpu.SemaphoreType.DMA((N_LOC,)),
            pltpu.SemaphoreType.REGULAR,
        ],
        compiler_params=pltpu.CompilerParams(collective_id=0, has_side_effects=True, vmem_limit_bytes=56 << 20),
        name="decoder_layer",
    )(
        queries[0], keys[0], values[0], residual[0], out_weight,
        w_gate[0].T, w_up[0].T, w_down[0], norm_gain[None],
        expert_ids[0].T, gate_weights[0].T, slots[0].T,
    )
    return both[:1], both[1:]


def solution(mesh):
    rows = P("exp", "ctx", None)
    placed = (rows, rows, rows, rows, P("ctx", None), P(), rows, rows, rows,
              P("exp", None, "ctx"), P("exp", None, "ctx"), rows)
    return jax.shard_map(shards, mesh=mesh, in_specs=placed, out_specs=(rows, rows), check_vma=False)
```

```python
import functools

import jax
import jax.numpy as jnp
from jax import lax
from jax.experimental import pallas as pl
from jax.experimental.pallas import tpu as pltpu
from jax.sharding import PartitionSpec as P

D = 4096
HD = 128
QH = 32
TOK = 128
NZ = 4
HEADS = QH // NZ
HW = HEADS * HD
SEQ = 1024
FF_DEV = 192
FF_CHIP = 2 * FF_DEV
K_DEV = 512
CAP = 4
ROWS = 64
SCALE_COLS = 128
NCH = 4
CW = D // NCH
DX = D + SCALE_COLS
HALF = D // 2
QW = HALF // 4
BLOCKS = 16
EW = CW // 4
STACK = 4 * ROWS
F32 = jnp.float32
BF16 = jnp.bfloat16
MESH = pl.DeviceIdType.MESH

NT = (((1,), (1,)), ((), ()))


def cols(j):
    return pl.ds(j * CW, CW)


def xcols(j):
    return pl.ds(j * CW, CW + (SCALE_COLS if j == NCH - 1 else 0))


def qcols(p):
    return pl.ds(p * QW, QW + (SCALE_COLS if p == 1 else 0))


_count = 0


def _take(n):
    global _count
    first = _count
    _count += n
    return first


S_Q = _take(7)
S_KV = _take(16)
S_FWD = _take(4)
S_W = _take(1)
S_EW = _take(3)
S_WZ = _take(4)
S_W1 = _take(16)
S_W2 = _take(16)
S_W3 = _take(16)
S_WF = _take(16)
S_P = _take(8)
S_OUT = _take(2 * BLOCKS)
S_G1 = _take(NCH)
S_G2 = _take(NCH)
S_G3 = _take(NCH)
S_RELAY2 = _take(6)
S_PLUS2 = _take(6)
S_MINUS2 = _take(6)
S_EARLY = _take(BLOCKS)
S_RELAY3 = _take(2)
S_PLUS3 = _take(2)
S_MINUS3 = _take(2)
S_BACK = _take(2 * BLOCKS)
N_SEM = _count

L_Q = 0
L_KV = 3
L_W = 7
L_G = 8
L_U = 9
L_D = 10
L_RES = 11
L_ATT = 12
L_OUT = L_ATT + NCH
N_LOC = L_OUT + NCH


def layer(
    q_in, k_in, v_in, res_in, w_in, g_in, u_in, d_in, gain_ref, ids_ref, gates_ref, slots_ref,
    both_out,
    qb, kv, wb, wa_part, wb_part, gub, db, res, heads, proj, send_a, send_b, recv_a, recv_b, att, lay,
    place, comb_hi, comb_lo, gain_b,
    disp, xr, xall, acc, hid, ypart, relay2, plus2, minus2, yb, eb,
    early, stacks, relay3, plus3, minus3,
    ssem, rsem, lsem, ready,
):
    ctx = lax.axis_index("ctx")
    ex = lax.axis_index("exp")
    z, c = ctx // 2, ctx % 2
    x, y = ex // 4, ex % 4

    za, zb, zc = z + 1 - 2 * lax.rem(z, 2), NZ - 1 - z, lax.rem(z + 2, NZ)
    dev_a, dev_b = (za * 2 + c, ex), (zb * 2 + c, ex)

    def at_z(d):
        return (lax.rem(z + d + NZ, NZ) * 2 + c, ex)

    def at_x(d):
        return (ctx, lax.rem(x + d + 4, 4) * 4 + y)

    def at_y(d):
        return (ctx, x * 4 + lax.rem(y + d + 4, 4))

    def at_xy(n, sign=1):
        return (ctx, lax.rem(x + sign * (n // 4) + 4, 4) * 4 + lax.rem(y + sign * (n % 4) + 4, 4))

    plane = sorted(range(1, BLOCKS), key=lambda n: -min(n // 4, 4 - n // 4) - min(n % 4, 4 - n % 4))

    other = (z * 2 + 1 - c, ex)

    barrier = pltpu.get_barrier_semaphore()
    peers = [other] + [at(d) for at in (at_z, at_x, at_y) for d in (1, 2, 3)]
    for peer in peers:
        pl.semaphore_signal(barrier, inc=1, device_id=peer, device_id_type=MESH)

    def local(src, dst, n):
        return pltpu.make_async_copy(src, dst, lsem.at[n])

    sent = []

    def remote(src, dst, n, dev):
        return pltpu.make_async_remote_copy(
            src_ref=src, dst_ref=dst, send_sem=ssem.at[n], recv_sem=rsem.at[n],
            device_id=dev, device_id_type=MESH,
        )

    def send(src, dst, n, dev):
        copy = remote(src, dst, n, dev)
        copy.start()
        sent.append(copy)
        return copy

    mine = (2 * z + c) * TOK
    my_rows = pl.ds(pl.multiple_of(mine, TOK), TOK)

    def kv_parts():
        for h in range(2):
            for i, src in enumerate((k_in, v_in)):
                yield 2 * h + i, src.at[:, pl.ds(h * HD, HD)], kv.at[h, my_rows, pl.ds(i * HD, HD)]

    own_kv = [local(src, dst, L_KV + n) for n, src, dst in kv_parts()]

    def q_lanes(group):
        return q_in.at[:, pl.ds(pl.multiple_of(group * HW, HW), HW)]

    own_q = [local(q_lanes(g), qb.at[slot], L_Q + i) for i, (slot, g) in enumerate(((1, z), (4, za), (5, zb)))]
    w_rows = pl.ds(pl.multiple_of(c * K_DEV, K_DEV), K_DEV)
    own_w = local(w_in, wb.at[w_rows], L_W)
    g_rows = pl.ds(pl.multiple_of(c * FF_DEV, FF_DEV), FF_DEV)
    u_rows = pl.ds(pl.multiple_of(FF_CHIP + c * FF_DEV, FF_DEV), FF_DEV)
    own_g = local(g_in, gub.at[g_rows], L_G)
    own_u = local(u_in, gub.at[u_rows], L_U)
    own_d = local(d_in, db.at[g_rows], L_D)
    own_res = local(res_in, res, L_RES)
    for copy in (*own_kv, *own_q, own_w, own_res, own_g, own_u, own_d):
        copy.start()

    pl.semaphore_wait(barrier, len(peers))
    for d in (1, 2, 3):
        pl.semaphore_signal(ready, inc=1, device_id=at_x(d), device_id_type=MESH)

    row0 = c * K_DEV

    def w_part(buf, first, count, rnd, lane=0, lanes=CW):
        return buf.at[pl.ds(pl.multiple_of(row0 + first, 32), count), pl.ds(rnd * CW + lane, lanes)]

    ways = (
        (wa_part, 0, dev_a, 4 * x + y, x, at_y, at_x),
        (wb_part, D // 2, dev_b, 4 * y + x, y, at_x, at_y),
    )

    def w_step0(rnd):
        for i, (buf, lane, dev, piece, _, _, _) in enumerate(ways):
            first = pl.multiple_of(32 * piece, 32)
            src = w_in.at[pl.ds(first, 32), pl.ds(lane + rnd * CW, CW)]
            yield remote(src, w_part(buf, first, 32, rnd), S_WZ + 2 * rnd + i, dev)

    def w_step1(rnd):
        for i, (buf, _, _, piece, _, at1, _) in enumerate(ways):
            for d in (2, 1, 3):
                ref = w_part(buf, 32 * piece, 32, rnd)
                yield remote(ref, ref, S_W1 + 8 * rnd + 4 * i + d, at1(d))

    def w_step2(rnd):
        for i, (buf, _, _, _, block, _, at2) in enumerate(ways):
            for d in (1, 3):
                ref = w_part(buf, 128 * block, 128, rnd)
                yield remote(ref, ref, S_W2 + 8 * rnd + 4 * i + d, at2(d))

    def w_step3(rnd):
        for i, (buf, _, _, _, block, _, at2) in enumerate(ways):
            for d in (1, 3):
                ref = w_part(buf, 128 * lax.rem(block + 4 - d, 4), 128, rnd, (d // 2) * (CW // 2), CW // 2)
                yield remote(ref, ref, S_W3 + 8 * rnd + 4 * i + d, at2(d))

    def w_swap(rnd, which):
        for i, (buf, _, _, _, block, _, _) in enumerate(ways):
            for d in which:
                ref = w_part(buf, 128 * lax.rem(block + 4 - d, 4), 128, rnd)
                yield remote(ref, ref, S_WF + 8 * rnd + 4 * i + d, other)

    def begin(copies):
        for copy in copies:
            copy.start()

    def arrive(copies):
        for copy in copies:
            copy.wait_recv()

    begin(w_step0(0))
    kv_copies = {
        d: [send(src, dst, S_KV + 4 * d + n, at_z(d)) for n, src, dst in kv_parts()] for d in (2, 1, 3)
    }
    begin(w_step0(1))
    q_copies = [
        send(q_lanes(group), qb.at[slot], S_Q + slot, dev)
        for slot, group, dev in ((0, zb, dev_b), (2, za, dev_a), (3, zc, dev_b), (6, zc, dev_a))
    ]
    w_copy = send(w_in, wb.at[w_rows], S_W, other)

    for h in range(2):
        kv[h, :, pl.ds(2 * HD, HD)] = jnp.ones((SEQ, HD), BF16)
    ids = ids_ref[...]
    slots = slots_ref[...]
    gates = gates_ref[...]
    dest = ((ids // 4 - x) & 3) * 64 + (((ids & 3) - y) & 3) * 16 + slots
    dest = jnp.where(slots >= 0, dest, -16)
    row = lax.broadcasted_iota(jnp.int32, (STACK, TOK), 0)
    for quarter in range(4):
        placing = jnp.zeros((STACK, TOK), F32)
        combine = jnp.zeros((STACK, TOK), F32)
        for k in range(8):
            hit = row == dest[k : k + 1] + 4 * quarter
            placing += jnp.where(hit, 1.0, 0.0)
            combine += jnp.where(hit, gates[k : k + 1], 0.0)
        place[quarter] = placing.astype(BF16)
        combine = combine.T
        high = combine.astype(BF16)
        comb_hi[quarter] = high
        comb_lo[quarter] = (combine - high.astype(F32)).astype(BF16)
    gain_b[...] = jnp.broadcast_to(gain_ref[...], (8, D))

    for copy in own_kv:
        copy.wait()
    kv_lanes = pl.ds(0, 2 * HD)
    fwd = [send(kv.at[:, my_rows, kv_lanes], kv.at[:, my_rows, kv_lanes], S_FWD, other)]
    arrive(w_step0(0))
    begin(w_step1(0))
    for d in (1, 3, 2):
        arrive(kv_copies[d])
        rows = pl.ds(pl.multiple_of((lax.rem(z - d + NZ, NZ) * 2 + c) * TOK, TOK), TOK)
        fwd.append(send(kv.at[:, rows, kv_lanes], kv.at[:, rows, kv_lanes], S_FWD + d, other))
    arrive(w_step0(1))
    begin(w_step1(1))
    arrive(w_step1(0))
    begin(w_step2(0))
    begin(w_swap(0, (0,)))
    ew_copies = (
        send(g_in, gub.at[g_rows], S_EW, other),
        send(u_in, gub.at[u_rows], S_EW + 1, other),
        send(d_in, db.at[g_rows], S_EW + 2, other),
    )
    arrive(fwd)

    scale = HD**-0.5

    def attend(slot, owner, head):
        limit = c * TOK + lax.broadcasted_iota(jnp.int32, (TOK, 2 * TOK), 0)
        seen = lax.broadcasted_iota(jnp.int32, (TOK, 2 * TOK), 1) <= limit
        for v in range(NZ):

            @pl.when(owner == v)
            def _():
                keys = kv[head, pl.ds(0, 2 * TOK * (v + 1)), pl.ds(0, HD)]
                vals = kv[head, pl.ds(0, 2 * TOK * (v + 1)), pl.ds(HD, 2 * HD)]
                for h in range(HEADS):
                    lanes = pl.ds(h * HD, HD)
                    s = lax.dot_general(qb[slot, :, lanes], keys, NT, preferred_element_type=F32)
                    tail = jnp.where(seen, s[:, 2 * TOK * v :], -jnp.inf)
                    s = tail if v == 0 else jnp.concatenate([s[:, : 2 * TOK * v], tail], axis=1)
                    top = jnp.max(s, axis=1, keepdims=True)
                    p = jnp.exp((s - top) * scale).astype(BF16)
                    o = jnp.dot(p, vals, preferred_element_type=F32)
                    heads[pl.ds(pl.multiple_of(slot * TOK, TOK), TOK), lanes] = (o[:, :HD] / o[:, HD:]).astype(BF16)

    order = (1, 4, 5, 0, 2, 3, 6)
    owners = (zb, z, za, zb, z, z, za)
    groups = (z, z, z, za, za, zb, zb)

    def choose(step, values):
        out = values[order[0]]
        for n in range(1, 7):
            out = jnp.where(step == n, values[order[n]], out)
        return out

    for copy in own_q:
        copy.wait()

    def step_body(step, _):
        slot = choose(step, tuple(range(7)))

        @pl.when(step >= 3)
        def _():
            pltpu.make_async_copy(qb.at[1], qb.at[slot], rsem.at[S_Q + slot]).wait()

        attend(slot, choose(step, owners), choose(step, groups) // 2)

        @pl.when(step == 2)
        def _():
            arrive(w_step2(0))
            begin(w_step3(0))
            begin(w_swap(0, (1, 3)))
            arrive(w_step1(1))
            begin(w_step2(1))
            begin(w_swap(1, (0,)))

        return 0

    lax.fori_loop(0, 7, step_body, 0)

    def p_a(j, i):
        lanes = pl.ds(j * CW + i * QW, QW)
        return remote(send_a.at[:, lanes], recv_a.at[:, lanes], S_P + 2 * j + i, dev_b)

    def p_b(j, i):
        lanes = pl.ds((j - 2) * CW + i * QW, QW)
        return remote(send_b.at[:, lanes], recv_b.at[:, lanes], S_P + 2 * j + i, dev_a)

    def project(rnd):
        for i in range(2):
            lanes = pl.ds(rnd * CW + i * QW, QW)
            out = jnp.dot(heads[pl.ds(0, 2 * TOK), :], wb[:, lanes], preferred_element_type=F32)
            out += jnp.dot(heads[pl.ds(3 * TOK, 2 * TOK), :], wa_part[:, lanes], preferred_element_type=F32)
            send_a[:, lanes] = out[:TOK].astype(BF16)
            p_a(rnd, i).start()
            proj[:, lanes] = out[TOK:]
            wide = pl.ds(D // 2 + rnd * CW + i * QW, QW)
            out = jnp.dot(heads[pl.ds(TOK, 2 * TOK), :], wb[:, wide], preferred_element_type=F32)
            out += jnp.dot(heads[pl.ds(5 * TOK, 2 * TOK), :], wb_part[:, lanes], preferred_element_type=F32)
            send_b[:, lanes] = out[TOK:].astype(BF16)
            p_b(2 + rnd, i).start()
            proj[:, wide] = out[:TOK]
            sent.extend([p_a(rnd, i), p_b(2 + rnd, i)])

    def pick(quarter, stacked_axis):
        shape = (ROWS, STACK) if stacked_axis else (STACK, ROWS)
        at = lax.broadcasted_iota(jnp.int32, shape, stacked_axis)
        slot_row = lax.broadcasted_iota(jnp.int32, shape, 1 - stacked_axis)
        return jnp.where(at == (slot_row // 4) * 16 + 4 * quarter + slot_row % 4, 1.0, 0.0).astype(BF16)

    own_res.wait()
    pl.semaphore_wait(ready, 3)
    square = jnp.zeros((TOK, 1), F32)
    own_copies = []

    def out_copy(p, n):
        rows = pl.ds(16 * n, 16)
        return remote(disp.at[rows, qcols(p)], xr.at[rows, qcols(p)], S_OUT + BLOCKS * p + n, at_xy(n))

    def g1(j):
        return remote(xall.at[pl.ds(0, ROWS), xcols(j)], xall.at[pl.ds(ROWS, ROWS), xcols(j)], S_G1 + j, at_z(1))

    def g3(j):
        return remote(xall.at[pl.ds(0, ROWS), xcols(j)], xall.at[pl.ds(3 * ROWS, ROWS), xcols(j)], S_G3 + j, at_z(-1))

    def g2(j):
        slot, way = (1, 1) if j < 2 else (3, -1)
        return remote(
            xall.at[pl.ds(slot * ROWS, ROWS), xcols(j)], xall.at[pl.ds(2 * ROWS, ROWS), xcols(j)], S_G2 + j, at_z(way)
        )

    def start(copies):
        for copy in copies:
            copy.start()
            sent.append(copy)

    def attended_chunk(j, square):
        for i in range(2):
            (p_a if j < 2 else p_b)(j, i).wait_recv()
        lanes = pl.ds((j % 2) * CW, CW)
        total = proj[:, cols(j)] + (recv_a if j < 2 else recv_b)[:, lanes].astype(F32)
        a = (res[:, cols(j)].astype(F32) + total).astype(BF16)
        att[:, cols(j)] = a
        copy = local(att.at[:, cols(j)], both_out.at[0, :, cols(j)], L_ATT + j)
        copy.start()
        own_copies.append(copy)
        a = a.astype(F32)
        square += jnp.sum(a * a, axis=1, keepdims=True)
        scaled = (a * gain_b[pl.ds(0, 1), cols(j)]).astype(BF16)
        return square, scaled

    def dispatch_half(p, square):
        stack = jnp.zeros((STACK, QW), F32)
        for j in (p, 2 + p):
            square, scaled = attended_chunk(j, square)
            for i in range(2):
                stack += jnp.dot(place[2 * (j // 2) + i], scaled[:, i * QW : (i + 1) * QW], preferred_element_type=F32)
        stack = stack.astype(BF16)
        disp[:, pl.ds(p * QW, QW)] = stack
        xr[pl.ds(0, 16), pl.ds(p * QW, QW)] = stack[:16]
        if p == 1:
            norm = lax.rsqrt(square * (1.0 / D) + 1e-06)
            norm = jnp.broadcast_to(norm, (TOK, SCALE_COLS))
            norm_hi = norm.astype(BF16).astype(F32)
            lane = lax.broadcasted_iota(jnp.int32, (TOK, SCALE_COLS), 1)
            both = jnp.where(lane < SCALE_COLS // 2, norm_hi, norm - norm_hi).astype(BF16)
            stack = jnp.dot(place[0], both, preferred_element_type=F32).astype(BF16)
            disp[:, pl.ds(2 * QW, SCALE_COLS)] = stack
            xr[pl.ds(0, 16), pl.ds(2 * QW, SCALE_COLS)] = stack[:16]
        start([out_copy(p, n) for n in plane])
        return square

    def gather_half(p):
        for n in plane:
            out_copy(p, n).wait_recv()
        stack = xr[:, pl.ds(p * QW, QW)]
        for quarter in range(4):
            rows = jnp.dot(pick(quarter, 1), stack, preferred_element_type=F32).astype(BF16)
            xall[pl.ds(0, ROWS), pl.ds((quarter // 2) * HALF + p * CW + (quarter % 2) * QW, QW)] = rows
        if p == 1:
            rows = jnp.dot(pick(0, 1), xr[:, pl.ds(2 * QW, SCALE_COLS)], preferred_element_type=F32).astype(BF16)
            xall[pl.ds(0, ROWS), pl.ds(D, SCALE_COLS)] = rows
        for j in (p, 2 + p):
            start([g1(j), g3(j)])

    def pass_chunk(j):
        (g1(j) if j < 2 else g3(j)).wait_recv()
        start([g2(j)])

    def gate_up_chunk(j):
        (g3(j) if j < 2 else g1(j)).wait_recv()
        g2(j).wait_recv()
        prod = lax.dot_general(xall[:, cols(j)], gub[:, cols(j)], NT, preferred_element_type=F32)
        acc[...] = prod if j == 0 else acc[...] + prod

    own_w.wait()
    w_copy.wait_recv()
    arrive(w_step3(0))
    begin(w_swap(0, (2,)))
    arrive(w_swap(0, (0, 1, 3, 2)))
    project(0)
    arrive(w_step2(1))
    begin(w_step3(1))
    begin(w_swap(1, (1, 3)))
    square = dispatch_half(0, square)
    arrive(w_step3(1))
    begin(w_swap(1, (2,)))
    arrive(w_swap(1, (0, 1, 3, 2)))
    project(1)
    for rnd in (0, 1):
        for copies in (w_step0(rnd), w_step1(rnd), w_step2(rnd), w_step3(rnd), w_swap(rnd, (0, 1, 2, 3))):
            sent.extend(copies)
    gather_half(0)
    square = dispatch_half(1, square)
    for j in (0, 2):
        pass_chunk(j)
    gather_half(1)
    own_g.wait()
    own_u.wait()
    own_d.wait()
    for copy in ew_copies:
        copy.wait_recv()
    for j in (0, 2):
        gate_up_chunk(j)
    for j in (1, 3):
        pass_chunk(j)
    for j in (1, 3):
        gate_up_chunk(j)

    sc = xall[:, pl.ds(D, SCALE_COLS)].astype(F32)
    sc = sc[:, 0:1] + sc[:, SCALE_COLS // 2 : SCALE_COLS // 2 + 1]
    gate = acc[:, pl.ds(0, FF_CHIP)] * sc
    upper = acc[:, pl.ds(FF_CHIP, FF_CHIP)] * sc
    hid[...] = (gate * jax.nn.sigmoid(gate) * upper).astype(BF16)

    def unit(u):
        return pl.ds(u * QW, QW)

    def q_relay2(u):
        return remote(
            ypart.at[pl.ds(2 * ROWS, ROWS), unit(u)], relay2.at[:, unit(u)], S_RELAY2 + u, at_z(1 if u % 2 == 0 else -1)
        )

    def q_plus2(u):
        return remote(ypart.at[pl.ds(ROWS, ROWS), unit(u)], plus2.at[:, unit(u)], S_PLUS2 + u, at_z(-1))

    def q_minus2(u):
        return remote(ypart.at[pl.ds(3 * ROWS, ROWS), unit(u)], minus2.at[:, unit(u)], S_MINUS2 + u, at_z(1))

    def early_copy(n):
        rows = pl.ds(16 * n, 16)
        return remote(early.at[rows], stacks.at[rows], S_EARLY + n, at_xy(n, -1))

    def third(half):
        return pl.ds(half * (EW // 2), EW // 2)

    def slot_lanes(slot, half):
        return pl.ds(slot * EW + half * (EW // 2), EW // 2)

    def r_relay(half):
        return remote(
            stacks.at[:, slot_lanes(2, half)], relay3.at[:, third(half)], S_RELAY3 + half, at_z(1 if half == 0 else -1)
        )

    def r_plus(half):
        return remote(stacks.at[:, slot_lanes(1, half)], plus3.at[:, third(half)], S_PLUS3 + half, at_z(-1))

    def r_minus(half):
        return remote(stacks.at[:, slot_lanes(3, half)], minus3.at[:, third(half)], S_MINUS3 + half, at_z(1))

    for j in range(NCH - 1):
        ypart[:, cols(j)] = jnp.dot(hid[...], db[:, cols(j)], preferred_element_type=F32).astype(BF16)
        start([q_relay2(2 * j), q_relay2(2 * j + 1)])
    start([q_plus2(0), q_minus2(1)])
    last = jnp.dot(hid[...], db[:, cols(NCH - 1)], preferred_element_type=F32).astype(BF16)
    for slot in range(NZ):
        stack = jnp.zeros((STACK, EW), F32)
        for quarter in range(4):
            rows = last[slot * ROWS : (slot + 1) * ROWS, quarter * EW : (quarter + 1) * EW]
            stack += jnp.dot(pick(quarter, 0), rows, preferred_element_type=F32)
        stack = stack.astype(BF16)
        early[:, pl.ds(slot * EW, EW)] = stack
        stacks[pl.ds(0, 16), pl.ds(slot * EW, EW)] = stack[:16]
    start([early_copy(n) for n in plane])
    for u in range(6):
        joined, copy, direct = (3, q_minus2, q_plus2) if u % 2 == 0 else (1, q_plus2, q_minus2)
        q_relay2(u).wait_recv()
        rows = pl.ds(joined * ROWS, ROWS)
        ypart[rows, unit(u)] = (ypart[rows, unit(u)].astype(F32) + relay2[:, unit(u)].astype(F32)).astype(BF16)
        start([copy(u)])
        if u >= 2:
            start([direct(u)])

    widths = (QW, EW)

    def back_copy(p, n):
        rows = pl.ds(16 * n, 16)
        lanes = pl.ds(p * QW, widths[p])
        return remote(yb.at[rows, lanes], eb.at[rows, lanes], S_BACK + BLOCKS * p + n, at_xy(n, -1))

    def return_part(p):
        width = widths[p]
        stack = jnp.zeros((STACK, width), F32)
        quarter = 0
        for u in ((0, 1, 2, 3), (4, 5))[p]:
            q_plus2(u).wait_recv()
            q_minus2(u).wait_recv()
            rows = (
                ypart[pl.ds(0, ROWS), unit(u)].astype(F32)
                + plus2[:, unit(u)].astype(F32)
                + minus2[:, unit(u)].astype(F32)
            ).astype(BF16)
            for i in range(QW // width):
                part = rows[:, i * width : (i + 1) * width]
                stack += jnp.dot(pick(quarter, 0), part, preferred_element_type=F32)
                quarter += 1
        stack = stack.astype(BF16)
        lanes = pl.ds(p * QW, width)
        yb[:, lanes] = stack
        eb[pl.ds(0, 16), lanes] = stack[:16]
        start([back_copy(p, n) for n in plane])

    def combine_stack(p, first, width, stack):
        for quarter in range(4):
            lanes = pl.ds(first + quarter * width, width)
            moe = jnp.dot(comb_hi[quarter], stack, preferred_element_type=F32)
            moe += jnp.dot(comb_lo[quarter], stack, preferred_element_type=F32)
            lay[:, lanes] = (att[:, lanes].astype(F32) + moe).astype(BF16)
        lanes = pl.ds(first, 4 * width)
        copy = local(lay.at[:, lanes], both_out.at[1, :, lanes], L_OUT + p)
        copy.start()
        own_copies.append(copy)

    def combine_part(p):
        for n in plane:
            back_copy(p, n).wait_recv()
        combine_stack(p, p * HALF, widths[p], eb[:, pl.ds(p * QW, widths[p])])

    return_part(0)
    for n in plane:
        early_copy(n).wait_recv()
    start([r_relay(0), r_relay(1), r_plus(0), r_minus(1)])
    return_part(1)
    for half, slot, copy in ((0, 3, r_minus), (1, 1, r_plus)):
        r_relay(half).wait_recv()
        lanes = slot_lanes(slot, half)
        stacks[:, lanes] = (stacks[:, lanes].astype(F32) + relay3[:, third(half)].astype(F32)).astype(BF16)
        start([copy(half)])
    combine_part(0)
    combine_part(1)
    for half in (0, 1):
        r_plus(half).wait_recv()
        r_minus(half).wait_recv()
    stack = (
        stacks[:, pl.ds(0, EW)].astype(F32) + plus3[...].astype(F32) + minus3[...].astype(F32)
    ).astype(BF16)
    combine_stack(2, 3 * CW, EW, stack)

    for copy in own_copies:
        copy.wait()
    for copy in sent:
        copy.wait_send()


def shards(
    queries, keys, values, residual, out_weight, norm_gain, expert_ids, gate_weights, slots, w_gate, w_up, w_down
):
    out = jax.ShapeDtypeStruct((2, TOK, D), BF16)
    hbm = pl.BlockSpec(memory_space=pl.ANY)
    vmem = pl.BlockSpec(memory_space=pltpu.VMEM)

    def buf(*shape, dtype=BF16):
        return pltpu.VMEM(shape, dtype)

    both = pl.pallas_call(
        layer,
        out_shape=out,
        in_specs=[hbm] * 8 + [vmem] * 4,
        out_specs=hbm,
        scratch_shapes=[
            buf(7, TOK, HW),
            buf(2, SEQ, 3 * HD),
            buf(2 * K_DEV, D),
            buf(2 * K_DEV, D // 2),
            buf(2 * K_DEV, D // 2),
            buf(2 * FF_CHIP, D),
            buf(FF_CHIP, D),
            buf(TOK, D),
            buf(7 * TOK, HW),
            buf(TOK, D, dtype=F32),
            buf(TOK, D // 2),
            buf(TOK, D // 2),
            buf(TOK, D // 2),
            buf(TOK, D // 2),
            buf(TOK, D),
            buf(TOK, D),
            buf(4, STACK, TOK),
            buf(4, TOK, STACK),
            buf(4, TOK, STACK),
            buf(8, D, dtype=F32),
            buf(STACK, 2 * QW + SCALE_COLS),
            buf(STACK, 2 * QW + SCALE_COLS),
            buf(NZ * ROWS, DX),
            buf(NZ * ROWS, 2 * FF_CHIP, dtype=F32),
            buf(NZ * ROWS, FF_CHIP),
            buf(NZ * ROWS, D),
            buf(ROWS, D),
            buf(ROWS, D),
            buf(ROWS, D),
            buf(STACK, 2 * QW),
            buf(STACK, 2 * QW),
            buf(STACK, 4 * EW),
            buf(STACK, 4 * EW),
            buf(STACK, EW),
            buf(STACK, EW),
            buf(STACK, EW),
            pltpu.SemaphoreType.DMA((N_SEM,)),
            pltpu.SemaphoreType.DMA((N_SEM,)),
            pltpu.SemaphoreType.DMA((N_LOC,)),
            pltpu.SemaphoreType.REGULAR,
        ],
        compiler_params=pltpu.CompilerParams(collective_id=0, has_side_effects=True, vmem_limit_bytes=56 << 20),
        name="decoder_layer",
    )(
        queries[0], keys[0], values[0], residual[0], out_weight,
        w_gate[0].T, w_up[0].T, w_down[0], norm_gain[None],
        expert_ids[0].T, gate_weights[0].T, slots[0].T,
    )
    return both[:1], both[1:]


def solution(mesh):
    rows = P("exp", "ctx", None)
    placed = (rows, rows, rows, rows, P("ctx", None), P(), rows, rows, rows,
              P("exp", None, "ctx"), P("exp", None, "ctx"), rows)
    return jax.shard_map(shards, mesh=mesh, in_specs=placed, out_specs=(rows, rows), check_vma=False)
```

```python
import functools

import jax
import jax.numpy as jnp
from jax import lax
from jax.experimental import pallas as pl
from jax.experimental.pallas import tpu as pltpu
from jax.sharding import PartitionSpec as P

D = 4096
HD = 128
QH = 32
TOK = 128
NZ = 4
HEADS = QH // NZ
HW = HEADS * HD
SEQ = 1024
FF_DEV = 192
FF_CHIP = 2 * FF_DEV
K_DEV = 512
CAP = 4
ROWS = 64
SCALE_COLS = 128
NCH = 4
CW = D // NCH
DX = D + SCALE_COLS
HALF = D // 2
QW = HALF // 4
BLOCKS = 16
EW = CW // 4
STACK = 4 * ROWS
F32 = jnp.float32
BF16 = jnp.bfloat16
MESH = pl.DeviceIdType.MESH

NT = (((1,), (1,)), ((), ()))


def cols(j):
    return pl.ds(j * CW, CW)


def xcols(j):
    return pl.ds(j * CW, CW + (SCALE_COLS if j == NCH - 1 else 0))


def qcols(p):
    return pl.ds(p * QW, QW + (SCALE_COLS if p == 1 else 0))


_count = 0


def _take(n):
    global _count
    first = _count
    _count += n
    return first


S_Q = _take(7)
S_KV = _take(16)
S_FWD = _take(4)
S_W = _take(1)
S_EW = _take(3)
S_WZ = _take(4)
S_W1 = _take(16)
S_W2 = _take(16)
S_W3 = _take(16)
S_WF = _take(16)
S_P = _take(8)
S_OUT = _take(2 * BLOCKS)
S_G1 = _take(NCH)
S_G2 = _take(NCH)
S_G3 = _take(NCH)
S_RELAY2 = _take(6)
S_PLUS2 = _take(6)
S_MINUS2 = _take(6)
S_EARLY = _take(BLOCKS)
S_RELAY3 = _take(2)
S_PLUS3 = _take(2)
S_MINUS3 = _take(2)
S_BACK = _take(2 * BLOCKS)
N_SEM = _count

L_Q = 0
L_KV = 3
L_W = 7
L_G = 8
L_U = 9
L_D = 10
L_RES = 11
L_ATT = 12
L_OUT = L_ATT + NCH
N_LOC = L_OUT + NCH


def layer(
    q_in, k_in, v_in, res_in, w_in, g_in, u_in, d_in, gain_ref, ids_ref, gates_ref, slots_ref,
    both_out,
    qb, kv, wb, wa_part, wb_part, gub, db, res, heads, proj, send_a, send_b, recv_a, recv_b, att, lay,
    place, comb_hi, comb_lo, gain_b,
    disp, xr, xall, acc, hid, ypart, relay2, plus2, minus2, yb, eb,
    early, stacks, relay3, plus3, minus3,
    ssem, rsem, lsem, ready,
):
    ctx = lax.axis_index("ctx")
    ex = lax.axis_index("exp")
    z, c = ctx // 2, ctx % 2
    x, y = ex // 4, ex % 4

    za, zb, zc = z + 1 - 2 * lax.rem(z, 2), NZ - 1 - z, lax.rem(z + 2, NZ)
    dev_a, dev_b = (za * 2 + c, ex), (zb * 2 + c, ex)

    def at_z(d):
        return (lax.rem(z + d + NZ, NZ) * 2 + c, ex)

    def at_x(d):
        return (ctx, lax.rem(x + d + 4, 4) * 4 + y)

    def at_y(d):
        return (ctx, x * 4 + lax.rem(y + d + 4, 4))

    def at_xy(n, sign=1):
        return (ctx, lax.rem(x + sign * (n // 4) + 4, 4) * 4 + lax.rem(y + sign * (n % 4) + 4, 4))

    plane = sorted(range(1, BLOCKS), key=lambda n: -min(n // 4, 4 - n // 4) - min(n % 4, 4 - n % 4))

    other = (z * 2 + 1 - c, ex)

    barrier = pltpu.get_barrier_semaphore()
    peers = [other] + [at(d) for at in (at_z, at_x, at_y) for d in (1, 2, 3)]
    for peer in peers:
        pl.semaphore_signal(barrier, inc=1, device_id=peer, device_id_type=MESH)

    def local(src, dst, n):
        return pltpu.make_async_copy(src, dst, lsem.at[n])

    sent = []

    def remote(src, dst, n, dev):
        return pltpu.make_async_remote_copy(
            src_ref=src, dst_ref=dst, send_sem=ssem.at[n], recv_sem=rsem.at[n],
            device_id=dev, device_id_type=MESH,
        )

    def send(src, dst, n, dev):
        copy = remote(src, dst, n, dev)
        copy.start()
        sent.append(copy)
        return copy

    mine = (2 * z + c) * TOK
    my_rows = pl.ds(pl.multiple_of(mine, TOK), TOK)

    def kv_parts():
        for h in range(2):
            for i, src in enumerate((k_in, v_in)):
                yield 2 * h + i, src.at[:, pl.ds(h * HD, HD)], kv.at[h, my_rows, pl.ds(i * HD, HD)]

    own_kv = [local(src, dst, L_KV + n) for n, src, dst in kv_parts()]

    def q_lanes(group):
        return q_in.at[:, pl.ds(pl.multiple_of(group * HW, HW), HW)]

    own_q = [local(q_lanes(g), qb.at[slot], L_Q + i) for i, (slot, g) in enumerate(((1, z), (4, za), (5, zb)))]
    w_rows = pl.ds(pl.multiple_of(c * K_DEV, K_DEV), K_DEV)
    own_w = local(w_in, wb.at[w_rows], L_W)
    g_rows = pl.ds(pl.multiple_of(c * FF_DEV, FF_DEV), FF_DEV)
    u_rows = pl.ds(pl.multiple_of(FF_CHIP + c * FF_DEV, FF_DEV), FF_DEV)
    own_g = local(g_in, gub.at[g_rows], L_G)
    own_u = local(u_in, gub.at[u_rows], L_U)
    own_d = local(d_in, db.at[g_rows], L_D)
    own_res = local(res_in, res, L_RES)
    for copy in (*own_kv, *own_q, own_w, own_res, own_g, own_u, own_d):
        copy.start()

    pl.semaphore_wait(barrier, len(peers))
    for d in (1, 2, 3):
        pl.semaphore_signal(ready, inc=1, device_id=at_x(d), device_id_type=MESH)

    row0 = c * K_DEV

    def w_part(buf, first, count, rnd, lane=0, lanes=CW):
        return buf.at[pl.ds(pl.multiple_of(row0 + first, 32), count), pl.ds(rnd * CW + lane, lanes)]

    ways = (
        (wa_part, 0, dev_a, 4 * x + y, x, at_y, at_x),
        (wb_part, D // 2, dev_b, 4 * y + x, y, at_x, at_y),
    )

    def w_step0(rnd):
        for i, (buf, lane, dev, piece, _, _, _) in enumerate(ways):
            first = pl.multiple_of(32 * piece, 32)
            src = w_in.at[pl.ds(first, 32), pl.ds(lane + rnd * CW, CW)]
            yield remote(src, w_part(buf, first, 32, rnd), S_WZ + 2 * rnd + i, dev)

    def w_step1(rnd):
        for i, (buf, _, _, piece, _, at1, _) in enumerate(ways):
            for d in (2, 1, 3):
                ref = w_part(buf, 32 * piece, 32, rnd)
                yield remote(ref, ref, S_W1 + 8 * rnd + 4 * i + d, at1(d))

    def w_step2(rnd):
        for i, (buf, _, _, _, block, _, at2) in enumerate(ways):
            for d in (1, 3):
                ref = w_part(buf, 128 * block, 128, rnd)
                yield remote(ref, ref, S_W2 + 8 * rnd + 4 * i + d, at2(d))

    def w_step3(rnd):
        for i, (buf, _, _, _, block, _, at2) in enumerate(ways):
            for d in (1, 3):
                ref = w_part(buf, 128 * lax.rem(block + 4 - d, 4), 128, rnd, (d // 2) * (CW // 2), CW // 2)
                yield remote(ref, ref, S_W3 + 8 * rnd + 4 * i + d, at2(d))

    def w_swap(rnd, which):
        for i, (buf, _, _, _, block, _, _) in enumerate(ways):
            for d in which:
                ref = w_part(buf, 128 * lax.rem(block + 4 - d, 4), 128, rnd)
                yield remote(ref, ref, S_WF + 8 * rnd + 4 * i + d, other)

    def begin(copies):
        for copy in copies:
            copy.start()

    def arrive(copies):
        for copy in copies:
            copy.wait_recv()

    begin(w_step0(0))
    begin(w_step0(1))
    kv_copies = {
        d: [send(src, dst, S_KV + 4 * d + n, at_z(d)) for n, src, dst in kv_parts()] for d in (2, 1, 3)
    }
    q_copies = [
        send(q_lanes(group), qb.at[slot], S_Q + slot, dev)
        for slot, group, dev in ((0, zb, dev_b), (2, za, dev_a), (3, zc, dev_b), (6, zc, dev_a))
    ]
    w_copy = send(w_in, wb.at[w_rows], S_W, other)

    for h in range(2):
        kv[h, :, pl.ds(2 * HD, HD)] = jnp.ones((SEQ, HD), BF16)
    ids = ids_ref[...]
    slots = slots_ref[...]
    gates = gates_ref[...]
    dest = ((ids // 4 - x) & 3) * 64 + (((ids & 3) - y) & 3) * 16 + slots
    dest = jnp.where(slots >= 0, dest, -16)
    row = lax.broadcasted_iota(jnp.int32, (STACK, TOK), 0)
    for quarter in range(4):
        placing = jnp.zeros((STACK, TOK), F32)
        combine = jnp.zeros((STACK, TOK), F32)
        for k in range(8):
            hit = row == dest[k : k + 1] + 4 * quarter
            placing += jnp.where(hit, 1.0, 0.0)
            combine += jnp.where(hit, gates[k : k + 1], 0.0)
        place[quarter] = placing.astype(BF16)
        combine = combine.T
        high = combine.astype(BF16)
        comb_hi[quarter] = high
        comb_lo[quarter] = (combine - high.astype(F32)).astype(BF16)
    gain_b[...] = jnp.broadcast_to(gain_ref[...], (8, D))

    for copy in own_kv:
        copy.wait()
    kv_lanes = pl.ds(0, 2 * HD)
    fwd = [send(kv.at[:, my_rows, kv_lanes], kv.at[:, my_rows, kv_lanes], S_FWD, other)]
    arrive(w_step0(0))
    begin(w_step1(0))
    arrive(w_step0(1))
    begin(w_step1(1))
    for d in (1, 3, 2):
        arrive(kv_copies[d])
        rows = pl.ds(pl.multiple_of((lax.rem(z - d + NZ, NZ) * 2 + c) * TOK, TOK), TOK)
        fwd.append(send(kv.at[:, rows, kv_lanes], kv.at[:, rows, kv_lanes], S_FWD + d, other))
    arrive(w_step1(0))
    begin(w_step2(0))
    begin(w_swap(0, (0,)))
    ew_copies = (
        send(g_in, gub.at[g_rows], S_EW, other),
        send(u_in, gub.at[u_rows], S_EW + 1, other),
        send(d_in, db.at[g_rows], S_EW + 2, other),
    )
    arrive(fwd)

    scale = HD**-0.5

    def attend(slot, owner, head):
        limit = c * TOK + lax.broadcasted_iota(jnp.int32, (TOK, 2 * TOK), 0)
        seen = lax.broadcasted_iota(jnp.int32, (TOK, 2 * TOK), 1) <= limit
        for v in range(NZ):

            @pl.when(owner == v)
            def _():
                keys = kv[head, pl.ds(0, 2 * TOK * (v + 1)), pl.ds(0, HD)]
                vals = kv[head, pl.ds(0, 2 * TOK * (v + 1)), pl.ds(HD, 2 * HD)]
                for h in range(HEADS):
                    lanes = pl.ds(h * HD, HD)
                    s = lax.dot_general(qb[slot, :, lanes], keys, NT, preferred_element_type=F32)
                    tail = jnp.where(seen, s[:, 2 * TOK * v :], -jnp.inf)
                    s = tail if v == 0 else jnp.concatenate([s[:, : 2 * TOK * v], tail], axis=1)
                    top = jnp.max(s, axis=1, keepdims=True)
                    p = jnp.exp((s - top) * scale).astype(BF16)
                    o = jnp.dot(p, vals, preferred_element_type=F32)
                    heads[pl.ds(pl.multiple_of(slot * TOK, TOK), TOK), lanes] = (o[:, :HD] / o[:, HD:]).astype(BF16)

    order = (1, 4, 5, 0, 2, 3, 6)
    owners = (zb, z, za, zb, z, z, za)
    groups = (z, z, z, za, za, zb, zb)

    def choose(step, values):
        out = values[order[0]]
        for n in range(1, 7):
            out = jnp.where(step == n, values[order[n]], out)
        return out

    for copy in own_q:
        copy.wait()

    def step_body(step, _):
        slot = choose(step, tuple(range(7)))

        @pl.when(step >= 3)
        def _():
            pltpu.make_async_copy(qb.at[1], qb.at[slot], rsem.at[S_Q + slot]).wait()

        attend(slot, choose(step, owners), choose(step, groups) // 2)

        @pl.when(step == 2)
        def _():
            arrive(w_step2(0))
            begin(w_step3(0))
            begin(w_swap(0, (1, 3)))
            arrive(w_step1(1))
            begin(w_step2(1))
            begin(w_swap(1, (0,)))

        return 0

    lax.fori_loop(0, 7, step_body, 0)

    def p_a(j, i):
        lanes = pl.ds(j * CW + i * QW, QW)
        return remote(send_a.at[:, lanes], recv_a.at[:, lanes], S_P + 2 * j + i, dev_b)

    def p_b(j, i):
        lanes = pl.ds((j - 2) * CW + i * QW, QW)
        return remote(send_b.at[:, lanes], recv_b.at[:, lanes], S_P + 2 * j + i, dev_a)

    def project(rnd):
        for i in range(2):
            lanes = pl.ds(rnd * CW + i * QW, QW)
            out = jnp.dot(heads[pl.ds(0, 2 * TOK), :], wb[:, lanes], preferred_element_type=F32)
            out += jnp.dot(heads[pl.ds(3 * TOK, 2 * TOK), :], wa_part[:, lanes], preferred_element_type=F32)
            send_a[:, lanes] = out[:TOK].astype(BF16)
            p_a(rnd, i).start()
            proj[:, lanes] = out[TOK:]
            wide = pl.ds(D // 2 + rnd * CW + i * QW, QW)
            out = jnp.dot(heads[pl.ds(TOK, 2 * TOK), :], wb[:, wide], preferred_element_type=F32)
            out += jnp.dot(heads[pl.ds(5 * TOK, 2 * TOK), :], wb_part[:, lanes], preferred_element_type=F32)
            send_b[:, lanes] = out[TOK:].astype(BF16)
            p_b(2 + rnd, i).start()
            proj[:, wide] = out[:TOK]
            sent.extend([p_a(rnd, i), p_b(2 + rnd, i)])

    def pick(quarter, stacked_axis):
        shape = (ROWS, STACK) if stacked_axis else (STACK, ROWS)
        at = lax.broadcasted_iota(jnp.int32, shape, stacked_axis)
        slot_row = lax.broadcasted_iota(jnp.int32, shape, 1 - stacked_axis)
        return jnp.where(at == (slot_row // 4) * 16 + 4 * quarter + slot_row % 4, 1.0, 0.0).astype(BF16)

    own_res.wait()
    pl.semaphore_wait(ready, 3)
    square = jnp.zeros((TOK, 1), F32)
    own_copies = []

    def out_copy(p, n):
        rows = pl.ds(16 * n, 16)
        return remote(disp.at[rows, qcols(p)], xr.at[rows, qcols(p)], S_OUT + BLOCKS * p + n, at_xy(n))

    def g1(j):
        return remote(xall.at[pl.ds(0, ROWS), xcols(j)], xall.at[pl.ds(ROWS, ROWS), xcols(j)], S_G1 + j, at_z(1))

    def g3(j):
        return remote(xall.at[pl.ds(0, ROWS), xcols(j)], xall.at[pl.ds(3 * ROWS, ROWS), xcols(j)], S_G3 + j, at_z(-1))

    def g2(j):
        slot, way = (1, 1) if j < 2 else (3, -1)
        return remote(
            xall.at[pl.ds(slot * ROWS, ROWS), xcols(j)], xall.at[pl.ds(2 * ROWS, ROWS), xcols(j)], S_G2 + j, at_z(way)
        )

    def start(copies):
        for copy in copies:
            copy.start()
            sent.append(copy)

    def attended_chunk(j, square):
        for i in range(2):
            (p_a if j < 2 else p_b)(j, i).wait_recv()
        lanes = pl.ds((j % 2) * CW, CW)
        total = proj[:, cols(j)] + (recv_a if j < 2 else recv_b)[:, lanes].astype(F32)
        a = (res[:, cols(j)].astype(F32) + total).astype(BF16)
        att[:, cols(j)] = a
        copy = local(att.at[:, cols(j)], both_out.at[0, :, cols(j)], L_ATT + j)
        copy.start()
        own_copies.append(copy)
        a = a.astype(F32)
        square += jnp.sum(a * a, axis=1, keepdims=True)
        scaled = (a * gain_b[pl.ds(0, 1), cols(j)]).astype(BF16)
        return square, scaled

    def dispatch_half(p, square):
        stack = jnp.zeros((STACK, QW), F32)
        for j in (p, 2 + p):
            square, scaled = attended_chunk(j, square)
            for i in range(2):
                stack += jnp.dot(place[2 * (j // 2) + i], scaled[:, i * QW : (i + 1) * QW], preferred_element_type=F32)
        stack = stack.astype(BF16)
        disp[:, pl.ds(p * QW, QW)] = stack
        xr[pl.ds(0, 16), pl.ds(p * QW, QW)] = stack[:16]
        if p == 1:
            norm = lax.rsqrt(square * (1.0 / D) + 1e-06)
            norm = jnp.broadcast_to(norm, (TOK, SCALE_COLS))
            norm_hi = norm.astype(BF16).astype(F32)
            lane = lax.broadcasted_iota(jnp.int32, (TOK, SCALE_COLS), 1)
            both = jnp.where(lane < SCALE_COLS // 2, norm_hi, norm - norm_hi).astype(BF16)
            stack = jnp.dot(place[0], both, preferred_element_type=F32).astype(BF16)
            disp[:, pl.ds(2 * QW, SCALE_COLS)] = stack
            xr[pl.ds(0, 16), pl.ds(2 * QW, SCALE_COLS)] = stack[:16]
        start([out_copy(p, n) for n in plane])
        return square

    def gather_half(p):
        for n in plane:
            out_copy(p, n).wait_recv()
        stack = xr[:, pl.ds(p * QW, QW)]
        for quarter in range(4):
            rows = jnp.dot(pick(quarter, 1), stack, preferred_element_type=F32).astype(BF16)
            xall[pl.ds(0, ROWS), pl.ds((quarter // 2) * HALF + p * CW + (quarter % 2) * QW, QW)] = rows
        if p == 1:
            rows = jnp.dot(pick(0, 1), xr[:, pl.ds(2 * QW, SCALE_COLS)], preferred_element_type=F32).astype(BF16)
            xall[pl.ds(0, ROWS), pl.ds(D, SCALE_COLS)] = rows
        for j in (p, 2 + p):
            start([g1(j), g3(j)])

    def pass_chunk(j):
        (g1(j) if j < 2 else g3(j)).wait_recv()
        start([g2(j)])

    def gate_up_chunk(j):
        (g3(j) if j < 2 else g1(j)).wait_recv()
        g2(j).wait_recv()
        prod = lax.dot_general(xall[:, cols(j)], gub[:, cols(j)], NT, preferred_element_type=F32)
        acc[...] = prod if j == 0 else acc[...] + prod

    own_w.wait()
    w_copy.wait_recv()
    arrive(w_step3(0))
    begin(w_swap(0, (2,)))
    arrive(w_swap(0, (0, 1, 3, 2)))
    project(0)
    arrive(w_step2(1))
    begin(w_step3(1))
    begin(w_swap(1, (1, 3)))
    square = dispatch_half(0, square)
    arrive(w_step3(1))
    begin(w_swap(1, (2,)))
    arrive(w_swap(1, (0, 1, 3, 2)))
    project(1)
    for rnd in (0, 1):
        for copies in (w_step0(rnd), w_step1(rnd), w_step2(rnd), w_step3(rnd), w_swap(rnd, (0, 1, 2, 3))):
            sent.extend(copies)
    gather_half(0)
    square = dispatch_half(1, square)
    for j in (0, 2):
        pass_chunk(j)
    gather_half(1)
    own_g.wait()
    own_u.wait()
    own_d.wait()
    for copy in ew_copies:
        copy.wait_recv()
    for j in (0, 2):
        gate_up_chunk(j)
    for j in (1, 3):
        pass_chunk(j)
    for j in (1, 3):
        gate_up_chunk(j)

    sc = xall[:, pl.ds(D, SCALE_COLS)].astype(F32)
    sc = sc[:, 0:1] + sc[:, SCALE_COLS // 2 : SCALE_COLS // 2 + 1]
    gate = acc[:, pl.ds(0, FF_CHIP)] * sc
    upper = acc[:, pl.ds(FF_CHIP, FF_CHIP)] * sc
    hid[...] = (gate * jax.nn.sigmoid(gate) * upper).astype(BF16)

    def unit(u):
        return pl.ds(u * QW, QW)

    def q_relay2(u):
        return remote(
            ypart.at[pl.ds(2 * ROWS, ROWS), unit(u)], relay2.at[:, unit(u)], S_RELAY2 + u, at_z(1 if u % 2 == 0 else -1)
        )

    def q_plus2(u):
        return remote(ypart.at[pl.ds(ROWS, ROWS), unit(u)], plus2.at[:, unit(u)], S_PLUS2 + u, at_z(-1))

    def q_minus2(u):
        return remote(ypart.at[pl.ds(3 * ROWS, ROWS), unit(u)], minus2.at[:, unit(u)], S_MINUS2 + u, at_z(1))

    def early_copy(n):
        rows = pl.ds(16 * n, 16)
        return remote(early.at[rows], stacks.at[rows], S_EARLY + n, at_xy(n, -1))

    def third(half):
        return pl.ds(half * (EW // 2), EW // 2)

    def slot_lanes(slot, half):
        return pl.ds(slot * EW + half * (EW // 2), EW // 2)

    def r_relay(half):
        return remote(
            stacks.at[:, slot_lanes(2, half)], relay3.at[:, third(half)], S_RELAY3 + half, at_z(1 if half == 0 else -1)
        )

    def r_plus(half):
        return remote(stacks.at[:, slot_lanes(1, half)], plus3.at[:, third(half)], S_PLUS3 + half, at_z(-1))

    def r_minus(half):
        return remote(stacks.at[:, slot_lanes(3, half)], minus3.at[:, third(half)], S_MINUS3 + half, at_z(1))

    for j in range(NCH - 1):
        ypart[:, cols(j)] = jnp.dot(hid[...], db[:, cols(j)], preferred_element_type=F32).astype(BF16)
        start([q_relay2(2 * j), q_relay2(2 * j + 1)])
    start([q_plus2(0), q_minus2(1)])
    last = jnp.dot(hid[...], db[:, cols(NCH - 1)], preferred_element_type=F32).astype(BF16)
    for slot in range(NZ):
        stack = jnp.zeros((STACK, EW), F32)
        for quarter in range(4):
            rows = last[slot * ROWS : (slot + 1) * ROWS, quarter * EW : (quarter + 1) * EW]
            stack += jnp.dot(pick(quarter, 0), rows, preferred_element_type=F32)
        stack = stack.astype(BF16)
        early[:, pl.ds(slot * EW, EW)] = stack
        stacks[pl.ds(0, 16), pl.ds(slot * EW, EW)] = stack[:16]
    start([early_copy(n) for n in plane])
    for u in range(6):
        joined, copy, direct = (3, q_minus2, q_plus2) if u % 2 == 0 else (1, q_plus2, q_minus2)
        q_relay2(u).wait_recv()
        rows = pl.ds(joined * ROWS, ROWS)
        ypart[rows, unit(u)] = (ypart[rows, unit(u)].astype(F32) + relay2[:, unit(u)].astype(F32)).astype(BF16)
        start([copy(u)])
        if u >= 2:
            start([direct(u)])

    widths = (QW, EW)

    def back_copy(p, n):
        rows = pl.ds(16 * n, 16)
        lanes = pl.ds(p * QW, widths[p])
        return remote(yb.at[rows, lanes], eb.at[rows, lanes], S_BACK + BLOCKS * p + n, at_xy(n, -1))

    def return_part(p):
        width = widths[p]
        stack = jnp.zeros((STACK, width), F32)
        quarter = 0
        for u in ((0, 1, 2, 3), (4, 5))[p]:
            q_plus2(u).wait_recv()
            q_minus2(u).wait_recv()
            rows = (
                ypart[pl.ds(0, ROWS), unit(u)].astype(F32)
                + plus2[:, unit(u)].astype(F32)
                + minus2[:, unit(u)].astype(F32)
            ).astype(BF16)
            for i in range(QW // width):
                part = rows[:, i * width : (i + 1) * width]
                stack += jnp.dot(pick(quarter, 0), part, preferred_element_type=F32)
                quarter += 1
        stack = stack.astype(BF16)
        lanes = pl.ds(p * QW, width)
        yb[:, lanes] = stack
        eb[pl.ds(0, 16), lanes] = stack[:16]
        start([back_copy(p, n) for n in plane])

    def combine_stack(p, first, width, stack):
        for quarter in range(4):
            lanes = pl.ds(first + quarter * width, width)
            moe = jnp.dot(comb_hi[quarter], stack, preferred_element_type=F32)
            moe += jnp.dot(comb_lo[quarter], stack, preferred_element_type=F32)
            lay[:, lanes] = (att[:, lanes].astype(F32) + moe).astype(BF16)
        lanes = pl.ds(first, 4 * width)
        copy = local(lay.at[:, lanes], both_out.at[1, :, lanes], L_OUT + p)
        copy.start()
        own_copies.append(copy)

    def combine_part(p):
        for n in plane:
            back_copy(p, n).wait_recv()
        combine_stack(p, p * HALF, widths[p], eb[:, pl.ds(p * QW, widths[p])])

    return_part(0)
    for n in plane:
        early_copy(n).wait_recv()
    start([r_relay(0), r_relay(1), r_plus(0), r_minus(1)])
    return_part(1)
    for half, slot, copy in ((0, 3, r_minus), (1, 1, r_plus)):
        r_relay(half).wait_recv()
        lanes = slot_lanes(slot, half)
        stacks[:, lanes] = (stacks[:, lanes].astype(F32) + relay3[:, third(half)].astype(F32)).astype(BF16)
        start([copy(half)])
    combine_part(0)
    combine_part(1)
    for half in (0, 1):
        r_plus(half).wait_recv()
        r_minus(half).wait_recv()
    stack = (
        stacks[:, pl.ds(0, EW)].astype(F32) + plus3[...].astype(F32) + minus3[...].astype(F32)
    ).astype(BF16)
    combine_stack(2, 3 * CW, EW, stack)

    for copy in own_copies:
        copy.wait()
    for copy in sent:
        copy.wait_send()


def shards(
    queries, keys, values, residual, out_weight, norm_gain, expert_ids, gate_weights, slots, w_gate, w_up, w_down
):
    out = jax.ShapeDtypeStruct((2, TOK, D), BF16)
    hbm = pl.BlockSpec(memory_space=pl.ANY)
    vmem = pl.BlockSpec(memory_space=pltpu.VMEM)

    def buf(*shape, dtype=BF16):
        return pltpu.VMEM(shape, dtype)

    both = pl.pallas_call(
        layer,
        out_shape=out,
        in_specs=[hbm] * 8 + [vmem] * 4,
        out_specs=hbm,
        scratch_shapes=[
            buf(7, TOK, HW),
            buf(2, SEQ, 3 * HD),
            buf(2 * K_DEV, D),
            buf(2 * K_DEV, D // 2),
            buf(2 * K_DEV, D // 2),
            buf(2 * FF_CHIP, D),
            buf(FF_CHIP, D),
            buf(TOK, D),
            buf(7 * TOK, HW),
            buf(TOK, D, dtype=F32),
            buf(TOK, D // 2),
            buf(TOK, D // 2),
            buf(TOK, D // 2),
            buf(TOK, D // 2),
            buf(TOK, D),
            buf(TOK, D),
            buf(4, STACK, TOK),
            buf(4, TOK, STACK),
            buf(4, TOK, STACK),
            buf(8, D, dtype=F32),
            buf(STACK, 2 * QW + SCALE_COLS),
            buf(STACK, 2 * QW + SCALE_COLS),
            buf(NZ * ROWS, DX),
            buf(NZ * ROWS, 2 * FF_CHIP, dtype=F32),
            buf(NZ * ROWS, FF_CHIP),
            buf(NZ * ROWS, D),
            buf(ROWS, D),
            buf(ROWS, D),
            buf(ROWS, D),
            buf(STACK, 2 * QW),
            buf(STACK, 2 * QW),
            buf(STACK, 4 * EW),
            buf(STACK, 4 * EW),
            buf(STACK, EW),
            buf(STACK, EW),
            buf(STACK, EW),
            pltpu.SemaphoreType.DMA((N_SEM,)),
            pltpu.SemaphoreType.DMA((N_SEM,)),
            pltpu.SemaphoreType.DMA((N_LOC,)),
            pltpu.SemaphoreType.REGULAR,
        ],
        compiler_params=pltpu.CompilerParams(collective_id=0, has_side_effects=True, vmem_limit_bytes=56 << 20),
        name="decoder_layer",
    )(
        queries[0], keys[0], values[0], residual[0], out_weight,
        w_gate[0].T, w_up[0].T, w_down[0], norm_gain[None],
        expert_ids[0].T, gate_weights[0].T, slots[0].T,
    )
    return both[:1], both[1:]


def solution(mesh):
    rows = P("exp", "ctx", None)
    placed = (rows, rows, rows, rows, P("ctx", None), P(), rows, rows, rows,
              P("exp", None, "ctx"), P("exp", None, "ctx"), rows)
    return jax.shard_map(shards, mesh=mesh, in_specs=placed, out_specs=(rows, rows), check_vma=False)
```

```python
import functools

import jax
import jax.numpy as jnp
from jax import lax
from jax.experimental import pallas as pl
from jax.experimental.pallas import tpu as pltpu
from jax.sharding import PartitionSpec as P

D = 4096
HD = 128
QH = 32
TOK = 128
NZ = 4
HEADS = QH // NZ
HW = HEADS * HD
SEQ = 1024
FF_DEV = 192
FF_CHIP = 2 * FF_DEV
K_DEV = 512
CAP = 4
ROWS = 64
SCALE_COLS = 128
NCH = 4
CW = D // NCH
DX = D + SCALE_COLS
HALF = D // 2
QW = HALF // 4
BLOCKS = 16
EW = CW // 4
STACK = 4 * ROWS
F32 = jnp.float32
BF16 = jnp.bfloat16
MESH = pl.DeviceIdType.MESH

NT = (((1,), (1,)), ((), ()))


def cols(j):
    return pl.ds(j * CW, CW)


def xcols(j):
    return pl.ds(j * CW, CW + (SCALE_COLS if j == NCH - 1 else 0))


def qcols(p):
    return pl.ds(p * QW, QW + (SCALE_COLS if p == 1 else 0))


_count = 0


def _take(n):
    global _count
    first = _count
    _count += n
    return first


S_Q = _take(7)
S_KV = _take(16)
S_FWD = _take(4)
S_W = _take(1)
S_EW = _take(3)
S_WZ = _take(4)
S_W1 = _take(16)
S_W2 = _take(16)
S_W3 = _take(16)
S_WF = _take(16)
S_P = _take(8)
S_OUT = _take(2 * BLOCKS)
S_G1 = _take(NCH)
S_G2 = _take(NCH)
S_G3 = _take(NCH)
S_RELAY2 = _take(6)
S_PLUS2 = _take(6)
S_MINUS2 = _take(6)
S_EARLY = _take(BLOCKS)
S_RELAY3 = _take(2)
S_PLUS3 = _take(2)
S_MINUS3 = _take(2)
S_BACK = _take(2 * BLOCKS)
N_SEM = _count

L_Q = 0
L_KV = 3
L_W = 7
L_G = 8
L_U = 9
L_D = 10
L_RES = 11
L_ATT = 12
L_OUT = L_ATT + NCH
N_LOC = L_OUT + NCH


def layer(
    q_in, k_in, v_in, res_in, w_in, g_in, u_in, d_in, gain_ref, ids_ref, gates_ref, slots_ref,
    both_out,
    qb, kv, wb, wa_part, wb_part, gub, db, res, heads, proj, send_a, send_b, recv_a, recv_b, att, lay,
    place, comb_hi, comb_lo, gain_b,
    disp, xr, xall, acc, hid, ypart, relay2, plus2, minus2, yb, eb,
    early, stacks, relay3, plus3, minus3,
    ssem, rsem, lsem, ready,
):
    ctx = lax.axis_index("ctx")
    ex = lax.axis_index("exp")
    z, c = ctx // 2, ctx % 2
    x, y = ex // 4, ex % 4

    za, zb, zc = z + 1 - 2 * lax.rem(z, 2), NZ - 1 - z, lax.rem(z + 2, NZ)
    dev_a, dev_b = (za * 2 + c, ex), (zb * 2 + c, ex)

    def at_z(d):
        return (lax.rem(z + d + NZ, NZ) * 2 + c, ex)

    def at_x(d):
        return (ctx, lax.rem(x + d + 4, 4) * 4 + y)

    def at_y(d):
        return (ctx, x * 4 + lax.rem(y + d + 4, 4))

    def at_xy(n, sign=1):
        return (ctx, lax.rem(x + sign * (n // 4) + 4, 4) * 4 + lax.rem(y + sign * (n % 4) + 4, 4))

    plane = sorted(range(1, BLOCKS), key=lambda n: -min(n // 4, 4 - n // 4) - min(n % 4, 4 - n % 4))

    other = (z * 2 + 1 - c, ex)

    barrier = pltpu.get_barrier_semaphore()
    peers = [other] + [at(d) for at in (at_z, at_x, at_y) for d in (1, 2, 3)]
    for peer in peers:
        pl.semaphore_signal(barrier, inc=1, device_id=peer, device_id_type=MESH)

    def local(src, dst, n):
        return pltpu.make_async_copy(src, dst, lsem.at[n])

    sent = []

    def remote(src, dst, n, dev):
        return pltpu.make_async_remote_copy(
            src_ref=src, dst_ref=dst, send_sem=ssem.at[n], recv_sem=rsem.at[n],
            device_id=dev, device_id_type=MESH,
        )

    def send(src, dst, n, dev):
        copy = remote(src, dst, n, dev)
        copy.start()
        sent.append(copy)
        return copy

    mine = (2 * z + c) * TOK
    my_rows = pl.ds(pl.multiple_of(mine, TOK), TOK)

    def kv_parts():
        for h in range(2):
            for i, src in enumerate((k_in, v_in)):
                yield 2 * h + i, src.at[:, pl.ds(h * HD, HD)], kv.at[h, my_rows, pl.ds(i * HD, HD)]

    own_kv = [local(src, dst, L_KV + n) for n, src, dst in kv_parts()]

    def q_lanes(group):
        return q_in.at[:, pl.ds(pl.multiple_of(group * HW, HW), HW)]

    own_q = [local(q_lanes(g), qb.at[slot], L_Q + i) for i, (slot, g) in enumerate(((1, z), (4, za), (5, zb)))]
    w_rows = pl.ds(pl.multiple_of(c * K_DEV, K_DEV), K_DEV)
    own_w = local(w_in, wb.at[w_rows], L_W)
    g_rows = pl.ds(pl.multiple_of(c * FF_DEV, FF_DEV), FF_DEV)
    u_rows = pl.ds(pl.multiple_of(FF_CHIP + c * FF_DEV, FF_DEV), FF_DEV)
    own_g = local(g_in, gub.at[g_rows], L_G)
    own_u = local(u_in, gub.at[u_rows], L_U)
    own_d = local(d_in, db.at[g_rows], L_D)
    own_res = local(res_in, res, L_RES)
    for copy in (*own_kv, *own_q, own_w, own_res, own_g, own_u, own_d):
        copy.start()

    pl.semaphore_wait(barrier, len(peers))
    for d in (1, 2, 3):
        pl.semaphore_signal(ready, inc=1, device_id=at_x(d), device_id_type=MESH)

    row0 = c * K_DEV

    def w_part(buf, first, count, rnd, lane=0, lanes=CW):
        return buf.at[pl.ds(pl.multiple_of(row0 + first, 32), count), pl.ds(rnd * CW + lane, lanes)]

    ways = (
        (wa_part, 0, dev_a, 4 * x + y, x, at_y, at_x),
        (wb_part, D // 2, dev_b, 4 * y + x, y, at_x, at_y),
    )

    def w_step0(rnd):
        for i, (buf, lane, dev, piece, _, _, _) in enumerate(ways):
            first = pl.multiple_of(32 * piece, 32)
            src = w_in.at[pl.ds(first, 32), pl.ds(lane + rnd * CW, CW)]
            yield remote(src, w_part(buf, first, 32, rnd), S_WZ + 2 * rnd + i, dev)

    def w_step1(rnd):
        for i, (buf, _, _, piece, _, at1, _) in enumerate(ways):
            for d in (2, 1, 3):
                ref = w_part(buf, 32 * piece, 32, rnd)
                yield remote(ref, ref, S_W1 + 8 * rnd + 4 * i + d, at1(d))

    def w_step2(rnd):
        for i, (buf, _, _, _, block, _, at2) in enumerate(ways):
            for d in (1, 3):
                ref = w_part(buf, 128 * block, 128, rnd)
                yield remote(ref, ref, S_W2 + 8 * rnd + 4 * i + d, at2(d))

    def w_step3(rnd):
        for i, (buf, _, _, _, block, _, at2) in enumerate(ways):
            for d in (1, 3):
                ref = w_part(buf, 128 * lax.rem(block + 4 - d, 4), 128, rnd, (d // 2) * (CW // 2), CW // 2)
                yield remote(ref, ref, S_W3 + 8 * rnd + 4 * i + d, at2(d))

    def w_swap(rnd, which):
        for i, (buf, _, _, _, block, _, _) in enumerate(ways):
            for d in which:
                ref = w_part(buf, 128 * lax.rem(block + 4 - d, 4), 128, rnd)
                yield remote(ref, ref, S_WF + 8 * rnd + 4 * i + d, other)

    def begin(copies):
        for copy in copies:
            copy.start()

    def arrive(copies):
        for copy in copies:
            copy.wait_recv()

    begin(w_step0(0))
    begin(w_step0(1))
    kv_copies = {
        d: [send(src, dst, S_KV + 4 * d + n, at_z(d)) for n, src, dst in kv_parts()] for d in (2, 1, 3)
    }
    q_copies = [
        send(q_lanes(group), qb.at[slot], S_Q + slot, dev)
        for slot, group, dev in ((0, zb, dev_b), (2, za, dev_a), (3, zc, dev_b), (6, zc, dev_a))
    ]
    w_copy = send(w_in, wb.at[w_rows], S_W, other)

    for h in range(2):
        kv[h, :, pl.ds(2 * HD, HD)] = jnp.ones((SEQ, HD), BF16)
    ids = ids_ref[...]
    slots = slots_ref[...]
    gates = gates_ref[...]
    dest = ((ids // 4 - x) & 3) * 64 + (((ids & 3) - y) & 3) * 16 + slots
    dest = jnp.where(slots >= 0, dest, -16)
    row = lax.broadcasted_iota(jnp.int32, (STACK, TOK), 0)
    for quarter in range(4):
        placing = jnp.zeros((STACK, TOK), F32)
        combine = jnp.zeros((STACK, TOK), F32)
        for k in range(8):
            hit = row == dest[k : k + 1] + 4 * quarter
            placing += jnp.where(hit, 1.0, 0.0)
            combine += jnp.where(hit, gates[k : k + 1], 0.0)
        place[quarter] = placing.astype(BF16)
        combine = combine.T
        high = combine.astype(BF16)
        comb_hi[quarter] = high
        comb_lo[quarter] = (combine - high.astype(F32)).astype(BF16)
    gain_b[...] = jnp.broadcast_to(gain_ref[...], (8, D))

    for copy in own_kv:
        copy.wait()
    kv_lanes = pl.ds(0, 2 * HD)
    fwd = [send(kv.at[:, my_rows, kv_lanes], kv.at[:, my_rows, kv_lanes], S_FWD, other)]
    arrive(w_step0(0))
    begin(w_step1(0))
    arrive(w_step0(1))
    begin(w_step1(1))
    for d in (1, 3, 2):
        arrive(kv_copies[d])
        rows = pl.ds(pl.multiple_of((lax.rem(z - d + NZ, NZ) * 2 + c) * TOK, TOK), TOK)
        fwd.append(send(kv.at[:, rows, kv_lanes], kv.at[:, rows, kv_lanes], S_FWD + d, other))
    arrive(w_step1(0))
    begin(w_step2(0))
    begin(w_swap(0, (0,)))
    arrive(fwd)

    scale = HD**-0.5

    def attend(slot, owner, head):
        limit = c * TOK + lax.broadcasted_iota(jnp.int32, (TOK, 2 * TOK), 0)
        seen = lax.broadcasted_iota(jnp.int32, (TOK, 2 * TOK), 1) <= limit
        for v in range(NZ):

            @pl.when(owner == v)
            def _():
                keys = kv[head, pl.ds(0, 2 * TOK * (v + 1)), pl.ds(0, HD)]
                vals = kv[head, pl.ds(0, 2 * TOK * (v + 1)), pl.ds(HD, 2 * HD)]
                for h in range(HEADS):
                    lanes = pl.ds(h * HD, HD)
                    s = lax.dot_general(qb[slot, :, lanes], keys, NT, preferred_element_type=F32)
                    tail = jnp.where(seen, s[:, 2 * TOK * v :], -jnp.inf)
                    s = tail if v == 0 else jnp.concatenate([s[:, : 2 * TOK * v], tail], axis=1)
                    top = jnp.max(s, axis=1, keepdims=True)
                    p = jnp.exp((s - top) * scale).astype(BF16)
                    o = jnp.dot(p, vals, preferred_element_type=F32)
                    heads[pl.ds(pl.multiple_of(slot * TOK, TOK), TOK), lanes] = (o[:, :HD] / o[:, HD:]).astype(BF16)

    order = (1, 4, 5, 0, 2, 3, 6)
    owners = (zb, z, za, zb, z, z, za)
    groups = (z, z, z, za, za, zb, zb)

    def choose(step, values):
        out = values[order[0]]
        for n in range(1, 7):
            out = jnp.where(step == n, values[order[n]], out)
        return out

    for copy in own_q:
        copy.wait()

    def step_body(step, _):
        slot = choose(step, tuple(range(7)))

        @pl.when(step >= 3)
        def _():
            pltpu.make_async_copy(qb.at[1], qb.at[slot], rsem.at[S_Q + slot]).wait()

        attend(slot, choose(step, owners), choose(step, groups) // 2)

        @pl.when(step == 2)
        def _():
            arrive(w_step2(0))
            begin(w_step3(0))
            begin(w_swap(0, (1, 3)))
            arrive(w_step1(1))
            begin(w_step2(1))
            begin(w_swap(1, (0,)))

        return 0

    lax.fori_loop(0, 7, step_body, 0)

    def p_a(j, i):
        lanes = pl.ds(j * CW + i * QW, QW)
        return remote(send_a.at[:, lanes], recv_a.at[:, lanes], S_P + 2 * j + i, dev_b)

    def p_b(j, i):
        lanes = pl.ds((j - 2) * CW + i * QW, QW)
        return remote(send_b.at[:, lanes], recv_b.at[:, lanes], S_P + 2 * j + i, dev_a)

    def project(rnd):
        for i in range(2):
            lanes = pl.ds(rnd * CW + i * QW, QW)
            out = jnp.dot(heads[pl.ds(0, 2 * TOK), :], wb[:, lanes], preferred_element_type=F32)
            out += jnp.dot(heads[pl.ds(3 * TOK, 2 * TOK), :], wa_part[:, lanes], preferred_element_type=F32)
            send_a[:, lanes] = out[:TOK].astype(BF16)
            p_a(rnd, i).start()
            proj[:, lanes] = out[TOK:]
            wide = pl.ds(D // 2 + rnd * CW + i * QW, QW)
            out = jnp.dot(heads[pl.ds(TOK, 2 * TOK), :], wb[:, wide], preferred_element_type=F32)
            out += jnp.dot(heads[pl.ds(5 * TOK, 2 * TOK), :], wb_part[:, lanes], preferred_element_type=F32)
            send_b[:, lanes] = out[TOK:].astype(BF16)
            p_b(2 + rnd, i).start()
            proj[:, wide] = out[:TOK]
            sent.extend([p_a(rnd, i), p_b(2 + rnd, i)])

    def pick(quarter, stacked_axis):
        shape = (ROWS, STACK) if stacked_axis else (STACK, ROWS)
        at = lax.broadcasted_iota(jnp.int32, shape, stacked_axis)
        slot_row = lax.broadcasted_iota(jnp.int32, shape, 1 - stacked_axis)
        return jnp.where(at == (slot_row // 4) * 16 + 4 * quarter + slot_row % 4, 1.0, 0.0).astype(BF16)

    own_res.wait()
    pl.semaphore_wait(ready, 3)
    square = jnp.zeros((TOK, 1), F32)
    own_copies = []

    def out_copy(p, n):
        rows = pl.ds(16 * n, 16)
        return remote(disp.at[rows, qcols(p)], xr.at[rows, qcols(p)], S_OUT + BLOCKS * p + n, at_xy(n))

    def g1(j):
        return remote(xall.at[pl.ds(0, ROWS), xcols(j)], xall.at[pl.ds(ROWS, ROWS), xcols(j)], S_G1 + j, at_z(1))

    def g3(j):
        return remote(xall.at[pl.ds(0, ROWS), xcols(j)], xall.at[pl.ds(3 * ROWS, ROWS), xcols(j)], S_G3 + j, at_z(-1))

    def g2(j):
        slot, way = (1, 1) if j < 2 else (3, -1)
        return remote(
            xall.at[pl.ds(slot * ROWS, ROWS), xcols(j)], xall.at[pl.ds(2 * ROWS, ROWS), xcols(j)], S_G2 + j, at_z(way)
        )

    def start(copies):
        for copy in copies:
            copy.start()
            sent.append(copy)

    def attended_chunk(j, square):
        for i in range(2):
            (p_a if j < 2 else p_b)(j, i).wait_recv()
        lanes = pl.ds((j % 2) * CW, CW)
        total = proj[:, cols(j)] + (recv_a if j < 2 else recv_b)[:, lanes].astype(F32)
        a = (res[:, cols(j)].astype(F32) + total).astype(BF16)
        att[:, cols(j)] = a
        copy = local(att.at[:, cols(j)], both_out.at[0, :, cols(j)], L_ATT + j)
        copy.start()
        own_copies.append(copy)
        a = a.astype(F32)
        square += jnp.sum(a * a, axis=1, keepdims=True)
        scaled = (a * gain_b[pl.ds(0, 1), cols(j)]).astype(BF16)
        return square, scaled

    def dispatch_half(p, square):
        stack = jnp.zeros((STACK, QW), F32)
        for j in (p, 2 + p):
            square, scaled = attended_chunk(j, square)
            for i in range(2):
                stack += jnp.dot(place[2 * (j // 2) + i], scaled[:, i * QW : (i + 1) * QW], preferred_element_type=F32)
        stack = stack.astype(BF16)
        disp[:, pl.ds(p * QW, QW)] = stack
        xr[pl.ds(0, 16), pl.ds(p * QW, QW)] = stack[:16]
        if p == 1:
            norm = lax.rsqrt(square * (1.0 / D) + 1e-06)
            norm = jnp.broadcast_to(norm, (TOK, SCALE_COLS))
            norm_hi = norm.astype(BF16).astype(F32)
            lane = lax.broadcasted_iota(jnp.int32, (TOK, SCALE_COLS), 1)
            both = jnp.where(lane < SCALE_COLS // 2, norm_hi, norm - norm_hi).astype(BF16)
            stack = jnp.dot(place[0], both, preferred_element_type=F32).astype(BF16)
            disp[:, pl.ds(2 * QW, SCALE_COLS)] = stack
            xr[pl.ds(0, 16), pl.ds(2 * QW, SCALE_COLS)] = stack[:16]
        start([out_copy(p, n) for n in plane])
        return square

    def gather_half(p):
        for n in plane:
            out_copy(p, n).wait_recv()
        stack = xr[:, pl.ds(p * QW, QW)]
        for quarter in range(4):
            rows = jnp.dot(pick(quarter, 1), stack, preferred_element_type=F32).astype(BF16)
            xall[pl.ds(0, ROWS), pl.ds((quarter // 2) * HALF + p * CW + (quarter % 2) * QW, QW)] = rows
        if p == 1:
            rows = jnp.dot(pick(0, 1), xr[:, pl.ds(2 * QW, SCALE_COLS)], preferred_element_type=F32).astype(BF16)
            xall[pl.ds(0, ROWS), pl.ds(D, SCALE_COLS)] = rows
        for j in (p, 2 + p):
            start([g1(j), g3(j)])

    def pass_chunk(j):
        (g1(j) if j < 2 else g3(j)).wait_recv()
        start([g2(j)])

    def gate_up_chunk(j):
        (g3(j) if j < 2 else g1(j)).wait_recv()
        g2(j).wait_recv()
        prod = lax.dot_general(xall[:, cols(j)], gub[:, cols(j)], NT, preferred_element_type=F32)
        acc[...] = prod if j == 0 else acc[...] + prod

    own_w.wait()
    w_copy.wait_recv()
    arrive(w_step3(0))
    begin(w_swap(0, (2,)))
    arrive(w_swap(0, (0, 1, 3, 2)))
    project(0)
    arrive(w_step2(1))
    begin(w_step3(1))
    begin(w_swap(1, (1, 3)))
    square = dispatch_half(0, square)
    arrive(w_step3(1))
    begin(w_swap(1, (2,)))
    arrive(w_swap(1, (0, 1, 3, 2)))
    project(1)
    ew_copies = (
        send(g_in, gub.at[g_rows], S_EW, other),
        send(u_in, gub.at[u_rows], S_EW + 1, other),
        send(d_in, db.at[g_rows], S_EW + 2, other),
    )
    for rnd in (0, 1):
        for copies in (w_step0(rnd), w_step1(rnd), w_step2(rnd), w_step3(rnd), w_swap(rnd, (0, 1, 2, 3))):
            sent.extend(copies)
    gather_half(0)
    square = dispatch_half(1, square)
    for j in (0, 2):
        pass_chunk(j)
    gather_half(1)
    own_g.wait()
    own_u.wait()
    own_d.wait()
    for copy in ew_copies:
        copy.wait_recv()
    for j in (0, 2):
        gate_up_chunk(j)
    for j in (1, 3):
        pass_chunk(j)
    for j in (1, 3):
        gate_up_chunk(j)

    sc = xall[:, pl.ds(D, SCALE_COLS)].astype(F32)
    sc = sc[:, 0:1] + sc[:, SCALE_COLS // 2 : SCALE_COLS // 2 + 1]
    gate = acc[:, pl.ds(0, FF_CHIP)] * sc
    upper = acc[:, pl.ds(FF_CHIP, FF_CHIP)] * sc
    hid[...] = (gate * jax.nn.sigmoid(gate) * upper).astype(BF16)

    def unit(u):
        return pl.ds(u * QW, QW)

    def q_relay2(u):
        return remote(
            ypart.at[pl.ds(2 * ROWS, ROWS), unit(u)], relay2.at[:, unit(u)], S_RELAY2 + u, at_z(1 if u % 2 == 0 else -1)
        )

    def q_plus2(u):
        return remote(ypart.at[pl.ds(ROWS, ROWS), unit(u)], plus2.at[:, unit(u)], S_PLUS2 + u, at_z(-1))

    def q_minus2(u):
        return remote(ypart.at[pl.ds(3 * ROWS, ROWS), unit(u)], minus2.at[:, unit(u)], S_MINUS2 + u, at_z(1))

    def early_copy(n):
        rows = pl.ds(16 * n, 16)
        return remote(early.at[rows], stacks.at[rows], S_EARLY + n, at_xy(n, -1))

    def third(half):
        return pl.ds(half * (EW // 2), EW // 2)

    def slot_lanes(slot, half):
        return pl.ds(slot * EW + half * (EW // 2), EW // 2)

    def r_relay(half):
        return remote(
            stacks.at[:, slot_lanes(2, half)], relay3.at[:, third(half)], S_RELAY3 + half, at_z(1 if half == 0 else -1)
        )

    def r_plus(half):
        return remote(stacks.at[:, slot_lanes(1, half)], plus3.at[:, third(half)], S_PLUS3 + half, at_z(-1))

    def r_minus(half):
        return remote(stacks.at[:, slot_lanes(3, half)], minus3.at[:, third(half)], S_MINUS3 + half, at_z(1))

    for j in range(NCH - 1):
        ypart[:, cols(j)] = jnp.dot(hid[...], db[:, cols(j)], preferred_element_type=F32).astype(BF16)
        start([q_relay2(2 * j), q_relay2(2 * j + 1)])
    start([q_plus2(0), q_minus2(1)])
    last = jnp.dot(hid[...], db[:, cols(NCH - 1)], preferred_element_type=F32).astype(BF16)
    for slot in range(NZ):
        stack = jnp.zeros((STACK, EW), F32)
        for quarter in range(4):
            rows = last[slot * ROWS : (slot + 1) * ROWS, quarter * EW : (quarter + 1) * EW]
            stack += jnp.dot(pick(quarter, 0), rows, preferred_element_type=F32)
        stack = stack.astype(BF16)
        early[:, pl.ds(slot * EW, EW)] = stack
        stacks[pl.ds(0, 16), pl.ds(slot * EW, EW)] = stack[:16]
    start([early_copy(n) for n in plane])
    for u in range(6):
        joined, copy, direct = (3, q_minus2, q_plus2) if u % 2 == 0 else (1, q_plus2, q_minus2)
        q_relay2(u).wait_recv()
        rows = pl.ds(joined * ROWS, ROWS)
        ypart[rows, unit(u)] = (ypart[rows, unit(u)].astype(F32) + relay2[:, unit(u)].astype(F32)).astype(BF16)
        start([copy(u)])
        if u >= 2:
            start([direct(u)])

    widths = (QW, EW)

    def back_copy(p, n):
        rows = pl.ds(16 * n, 16)
        lanes = pl.ds(p * QW, widths[p])
        return remote(yb.at[rows, lanes], eb.at[rows, lanes], S_BACK + BLOCKS * p + n, at_xy(n, -1))

    def return_part(p):
        width = widths[p]
        stack = jnp.zeros((STACK, width), F32)
        quarter = 0
        for u in ((0, 1, 2, 3), (4, 5))[p]:
            q_plus2(u).wait_recv()
            q_minus2(u).wait_recv()
            rows = (
                ypart[pl.ds(0, ROWS), unit(u)].astype(F32)
                + plus2[:, unit(u)].astype(F32)
                + minus2[:, unit(u)].astype(F32)
            ).astype(BF16)
            for i in range(QW // width):
                part = rows[:, i * width : (i + 1) * width]
                stack += jnp.dot(pick(quarter, 0), part, preferred_element_type=F32)
                quarter += 1
        stack = stack.astype(BF16)
        lanes = pl.ds(p * QW, width)
        yb[:, lanes] = stack
        eb[pl.ds(0, 16), lanes] = stack[:16]
        start([back_copy(p, n) for n in plane])

    def combine_stack(p, first, width, stack):
        for quarter in range(4):
            lanes = pl.ds(first + quarter * width, width)
            moe = jnp.dot(comb_hi[quarter], stack, preferred_element_type=F32)
            moe += jnp.dot(comb_lo[quarter], stack, preferred_element_type=F32)
            lay[:, lanes] = (att[:, lanes].astype(F32) + moe).astype(BF16)
        lanes = pl.ds(first, 4 * width)
        copy = local(lay.at[:, lanes], both_out.at[1, :, lanes], L_OUT + p)
        copy.start()
        own_copies.append(copy)

    def combine_part(p):
        for n in plane:
            back_copy(p, n).wait_recv()
        combine_stack(p, p * HALF, widths[p], eb[:, pl.ds(p * QW, widths[p])])

    return_part(0)
    for n in plane:
        early_copy(n).wait_recv()
    start([r_relay(0), r_relay(1), r_plus(0), r_minus(1)])
    return_part(1)
    for half, slot, copy in ((0, 3, r_minus), (1, 1, r_plus)):
        r_relay(half).wait_recv()
        lanes = slot_lanes(slot, half)
        stacks[:, lanes] = (stacks[:, lanes].astype(F32) + relay3[:, third(half)].astype(F32)).astype(BF16)
        start([copy(half)])
    combine_part(0)
    combine_part(1)
    for half in (0, 1):
        r_plus(half).wait_recv()
        r_minus(half).wait_recv()
    stack = (
        stacks[:, pl.ds(0, EW)].astype(F32) + plus3[...].astype(F32) + minus3[...].astype(F32)
    ).astype(BF16)
    combine_stack(2, 3 * CW, EW, stack)

    for copy in own_copies:
        copy.wait()
    for copy in sent:
        copy.wait_send()


def shards(
    queries, keys, values, residual, out_weight, norm_gain, expert_ids, gate_weights, slots, w_gate, w_up, w_down
):
    out = jax.ShapeDtypeStruct((2, TOK, D), BF16)
    hbm = pl.BlockSpec(memory_space=pl.ANY)
    vmem = pl.BlockSpec(memory_space=pltpu.VMEM)

    def buf(*shape, dtype=BF16):
        return pltpu.VMEM(shape, dtype)

    both = pl.pallas_call(
        layer,
        out_shape=out,
        in_specs=[hbm] * 8 + [vmem] * 4,
        out_specs=hbm,
        scratch_shapes=[
            buf(7, TOK, HW),
            buf(2, SEQ, 3 * HD),
            buf(2 * K_DEV, D),
            buf(2 * K_DEV, D // 2),
            buf(2 * K_DEV, D // 2),
            buf(2 * FF_CHIP, D),
            buf(FF_CHIP, D),
            buf(TOK, D),
            buf(7 * TOK, HW),
            buf(TOK, D, dtype=F32),
            buf(TOK, D // 2),
            buf(TOK, D // 2),
            buf(TOK, D // 2),
            buf(TOK, D // 2),
            buf(TOK, D),
            buf(TOK, D),
            buf(4, STACK, TOK),
            buf(4, TOK, STACK),
            buf(4, TOK, STACK),
            buf(8, D, dtype=F32),
            buf(STACK, 2 * QW + SCALE_COLS),
            buf(STACK, 2 * QW + SCALE_COLS),
            buf(NZ * ROWS, DX),
            buf(NZ * ROWS, 2 * FF_CHIP, dtype=F32),
            buf(NZ * ROWS, FF_CHIP),
            buf(NZ * ROWS, D),
            buf(ROWS, D),
            buf(ROWS, D),
            buf(ROWS, D),
            buf(STACK, 2 * QW),
            buf(STACK, 2 * QW),
            buf(STACK, 4 * EW),
            buf(STACK, 4 * EW),
            buf(STACK, EW),
            buf(STACK, EW),
            buf(STACK, EW),
            pltpu.SemaphoreType.DMA((N_SEM,)),
            pltpu.SemaphoreType.DMA((N_SEM,)),
            pltpu.SemaphoreType.DMA((N_LOC,)),
            pltpu.SemaphoreType.REGULAR,
        ],
        compiler_params=pltpu.CompilerParams(collective_id=0, has_side_effects=True, vmem_limit_bytes=56 << 20),
        name="decoder_layer",
    )(
        queries[0], keys[0], values[0], residual[0], out_weight,
        w_gate[0].T, w_up[0].T, w_down[0], norm_gain[None],
        expert_ids[0].T, gate_weights[0].T, slots[0].T,
    )
    return both[:1], both[1:]


def solution(mesh):
    rows = P("exp", "ctx", None)
    placed = (rows, rows, rows, rows, P("ctx", None), P(), rows, rows, rows,
              P("exp", None, "ctx"), P("exp", None, "ctx"), rows)
    return jax.shard_map(shards, mesh=mesh, in_specs=placed, out_specs=(rows, rows), check_vma=False)
```
